256 devices in a mesh: dp: 4 (over y_hi, core), ctx: 8 (over y_lo, x), fsdp: 8 (over z).
Axes of the slice: x: 4, y: 4 (y_hi: 2, y_lo: 2; y = y_hi * 2 + y_lo), z: 8, core: 2. Of those that a mesh axis runs over, the one named last changes fastest.
Arguments:
- layer_in: bfloat16 [128, 1024, 1024], P(('dp', 'fsdp'), 'ctx'), may hold values from -6 to 6
- repack_plan: int32 [128], P(('dp', 'fsdp')), may hold values from 0 to 3, as said below
- lengths: int32 [128], P(('dp', 'fsdp')), may hold values from 1 to 1024, 65536 in all
- stamps: int32 [128, 1024], P(('dp', 'fsdp'), 'ctx'), may hold values from 0 to 255, as said below
- w_in: bfloat16 [1024, 2048], P('fsdp'), may hold values from -0.1875 to 0.1875
- w_out: bfloat16 [512, 1024], P('fsdp'), may hold values from -0.25 to 0.25
- time_bias: bfloat16 [2, 128], replicated, may hold values from -4 to 4
- grad_out: bfloat16 [128, 1024, 1024], P(('dp', 'fsdp'), 'ctx'), may hold values from -6 to 6
Outputs:
- input_gradient: bfloat16 [128, 1024, 1024], P(('dp', 'fsdp'), 'ctx')
- grad_w_in: float32 [1024, 2048], P('fsdp')
- grad_w_out: float32 [512, 1024], P('fsdp')
- grad_bias: float32 [2, 128], replicated
The draws below stay inside these ranges and needn't reach their ends.
Inputs may be any that keep to these rules, and one draw needn't show every extreme that they name: `repack_plan`: each aligned block of 4 entries (one device's) is a permutation of 0 to 3. `stamps`: nondecreasing along each history, and 255 at its last position. `lengths`: one history has exactly 1024 events.
All inputs are finite; a program needn't handle non-finite values. No bound on the sum of `lengths` on one device may be relied on, other than what follows from the above.
Results may differ from the reference program's by a relative error of at most 0.025.
Values may be sent and summed in bfloat16 or wider, within the bound.
No kernel may reach another device: no remote copies, remote signals or barrier semaphores. Data moves between devices by JAX's collectives and lax.ppermute only.
A program may use at most 128 MiB of HBM per device.

```python
import math
import jax
import jax.numpy as jnp
import numpy as np
from jax import lax

D = 1024
H = 2
DH = 256
NB = 128
S_DEV = 128
SEQ_DEV = 4
DA = 512
L = 1024
NSEQ = 128
N_DP = 4
N_CTX = 8
N_FSDP = 8


def draw_repack_plan(key, part):
    groups = NSEQ // SEQ_DEV
    keys = jax.random.split(key, groups)
    orders = jax.vmap(lambda single: jax.random.permutation(single, SEQ_DEV))(keys)
    return orders.reshape(NSEQ).astype(jnp.int32)


def draw_stamps(key, part):
    increments = jax.random.randint(key, (NSEQ, L), 0, 2).astype(jnp.int32)
    running = jnp.cumsum(increments, axis=1)
    final = jnp.maximum(running[:, -1:], 1)
    return (running * 255 // final).astype(jnp.int32)


def steps_of(own_key, shape, cuts, smallest, top_value):
    factor_of, own = 1.0, jax.random.fold_in(own_key, 6)
    for dim, shards_of in cuts:
        heights = jnp.exp(jax.random.uniform(jax.random.fold_in(own, dim), (shards_of,), jnp.float32, smallest / len(cuts), top_value / len(cuts)))
        factor_of = factor_of * jnp.repeat(heights, shape[dim] // shards_of).reshape([-1 if axis == dim else 1 for axis in range(len(shape))])
    return factor_of


def length_profile(count, total, reach, slope):
    loads = [(1 << 20) // math.isqrt(rank ** slope) + 1 for rank in range(2, count + 1)]
    spare, given = total - reach - (count - 1), [1] * (count - 1)
    while spare > 0:
        movable = [i for i in range(count - 1) if given[i] < reach]
        whole, remaining = sum([loads[i] for i in movable]), spare
        for i in movable:
            addition = min(reach - given[i], max(1, remaining * loads[i] // whole), spare)
            given[i] = given[i] + addition
            spare = spare - addition
    return np.array([reach] + given)


def uneven_parts(rng, number_of, total, most, lean):
    if number_of == 2:
        one = jax.random.randint(rng, (), max(1, total - most), min(most, total - 1) + 1)
        return jnp.stack([one, total - one])
    tallies = jnp.asarray(length_profile(number_of, total, most, lean), jnp.int32)
    twos = (number_of - 1) // 2
    giver, receiver = tallies[1:1 + 2 * twos:2], tallies[2:2 + 2 * twos:2]
    room = jnp.minimum(giver - 1, most - receiver)
    moved = jax.random.randint(jax.random.fold_in(rng, 1), (twos,), 0, 1 << 20) % (room + 1)
    tallies = tallies.at[1:1 + 2 * twos:2].set(giver - moved).at[2:2 + 2 * twos:2].set(receiver + moved)
    return tallies[jax.random.permutation(jax.random.fold_in(rng, 2), number_of)]


def scatter_about(stream_key, shape, scale, bound, cuts=(), kind=jnp.bfloat16):
    result = scale * jax.random.normal(stream_key, shape, jnp.float32)
    if cuts:
        result = result * steps_of(stream_key, shape, cuts, -0.22, 0.18)
    return jnp.clip(result, -bound, bound).astype(kind)


def setup_inputs(seed: int = 0) -> dict:
    key_of = jax.random.split(jax.random.key(seed), 9)
    layer_in = scatter_about(key_of[0], (NSEQ, L, D), 1.0, 6.0, ((0, 32), (1, 8)))
    repack_plan = draw_repack_plan(jax.random.fold_in(key_of[8], 71), 0)
    lengths = uneven_parts(key_of[2], NSEQ, NSEQ * L // 2, L, 2).astype(jnp.int32)
    stamps = draw_stamps(jax.random.fold_in(key_of[8], 71), 0)
    w_in = scatter_about(key_of[4], (D, 4 * DA), D ** -0.5, 0.1875, ((0, 8),))
    w_out = scatter_about(key_of[5], (DA, D), DA ** -0.5, 0.25, ((0, 8),))
    time_bias = scatter_about(key_of[6], (H, NB), 1.0, 4.0)
    grad_out = scatter_about(key_of[7], (NSEQ, L, D), 1.0, 6.0, ((0, 32), (1, 8)))
    return {"layer_in": layer_in, "repack_plan": repack_plan, "lengths": lengths, "stamps": stamps, "w_in": w_in, "w_out": w_out, "time_bias": time_bias, "grad_out": grad_out}


EPS = 1e-05

def layer_normalize(values):
    centred = values - lax.optimization_barrier(jnp.mean(values, axis=-1, keepdims=True))
    inverse_permutation = lax.rsqrt(lax.optimization_barrier(jnp.mean(centred * centred, axis=-1, keepdims=True)) + EPS)
    return (centred * inverse_permutation, inverse_permutation)

def normalize_backward(grad, normalized_rows, inverse_permutation):
    return inverse_permutation * (grad - lax.optimization_barrier(jnp.mean(grad, axis=-1, keepdims=True)) - normalized_rows * lax.optimization_barrier(jnp.mean(grad * normalized_rows, axis=-1, keepdims=True)))

def silu_slope(values):
    sigma = jax.nn.sigmoid(values)
    return sigma * (1.0 + values * (1.0 - sigma))

def rounded_sum(parts):
    lowered = lax.optimization_barrier(parts.astype(jnp.bfloat16))
    return lax.optimization_barrier(jnp.sum(lowered.astype(jnp.float32), axis=0))

def one_history(layer_inputs, upstream, length, times, w_in, w_out, time_bias):
    events = layer_inputs.shape[0]
    attn_width = H * DH
    scale = DH ** (-0.5)
    centred_scaled, inverse_permutation = layer_normalize(layer_inputs.astype(jnp.float32))
    normalized_rows = centred_scaled.astype(jnp.bfloat16)
    hidden = jnp.dot(normalized_rows, w_in, preferred_element_type=jnp.float32)
    active = jax.nn.silu(hidden).astype(jnp.bfloat16)
    gate_u = active[:, :attn_width].astype(jnp.float32)
    values = active[:, attn_width:2 * attn_width].astype(jnp.float32).reshape(events, H, DH)
    query = active[:, 2 * attn_width:3 * attn_width].astype(jnp.float32).reshape(events, H, DH)
    keyset = active[:, 3 * attn_width:].astype(jnp.float32).reshape(events, H, DH)
    position = jnp.arange(events, dtype=jnp.int32)
    live = ((position[None, :] <= position[:, None]) & (position[:, None] < length)).astype(jnp.float32)
    bucket = jnp.clip(times[:, None] - times[None, :], 0, NB - 1).astype(jnp.int32)
    bias = time_bias.astype(jnp.float32)[:, bucket]
    scores = scale * jnp.einsum('ihd,jhd->hij', query, keyset) + bias
    probs = (jax.nn.silu(scores) * live[None]).astype(jnp.bfloat16)
    mixed = jnp.einsum('hij,jhd->ihd', probs.astype(jnp.float32), values).reshape(events, attn_width)
    gated = mixed * gate_u
    zhat, ginv = layer_normalize(gated)
    zlow = zhat.astype(jnp.bfloat16)
    dz = jnp.dot(upstream, w_out.T, preferred_element_type=jnp.float32)
    dgated = normalize_backward(dz, zhat, ginv)
    datt = (dgated * gate_u).astype(jnp.bfloat16)
    dgate_u = dgated * mixed
    datt_heads = datt.astype(jnp.float32).reshape(events, H, DH)
    dprob = jnp.einsum('ihd,jhd->hij', datt_heads, values)
    dlow = (dprob * silu_slope(scores) * live[None]).astype(jnp.bfloat16)
    dlow_f = dlow.astype(jnp.float32)
    dquery = (scale * jnp.einsum('hij,jhd->ihd', dlow_f, keyset)).reshape(events, attn_width)
    prob_blocks = probs.astype(jnp.float32).reshape(H, N_CTX, S_DEV, events)
    slope_blocks = dlow_f.reshape(H, N_CTX, S_DEV, events)
    dvalue = rounded_sum(jnp.einsum('hcij,cihd->cjhd', prob_blocks, datt_heads.reshape(N_CTX, S_DEV, H, DH))).reshape(events, attn_width)
    dkey = rounded_sum(scale * jnp.einsum('hcij,cihd->cjhd', slope_blocks, query.reshape(N_CTX, S_DEV, H, DH))).reshape(events, attn_width)
    flat_bucket = bucket.reshape(-1)
    dbias = jax.vmap(lambda head_grad: jax.ops.segment_sum(head_grad.reshape(-1), flat_bucket, NB))(dlow_f)
    dact = jnp.concatenate([dgate_u, dvalue, dquery, dkey], axis=1)
    dhid = (dact * silu_slope(hidden)).astype(jnp.bfloat16)
    normalized_grad = jnp.dot(dhid, w_in.T, preferred_element_type=jnp.float32)
    input_gradient = normalize_backward(normalized_grad, centred_scaled, inverse_permutation).astype(jnp.bfloat16)
    return (input_gradient, normalized_rows, dhid, zlow, dbias)

def reference(layer_in, repack_plan, lengths, stamps, w_in, w_out, time_bias, grad_out):
    per_peer = SEQ_DEV // N_DP
    groups = NSEQ // SEQ_DEV
    local = jnp.arange(SEQ_DEV, dtype=jnp.int32)

    def group_step(carry, group):
        acc_in, acc_out, acc_bias = carry
        dest_dp = group // N_FSDP
        fsdp_index = group % N_FSDP
        source_group = local // per_peer * N_FSDP + fsdp_index
        source = source_group * SEQ_DEV + repack_plan[source_group * SEQ_DEV + dest_dp * per_peer + local % per_peer]
        history_in = layer_in[source]
        begin = (group * SEQ_DEV).astype(jnp.int32)
        upstream = lax.dynamic_slice_in_dim(grad_out, begin, SEQ_DEV, 0)
        lens = lax.dynamic_slice_in_dim(lengths, begin, SEQ_DEV, 0)
        times = lax.dynamic_slice_in_dim(stamps, begin, SEQ_DEV, 0)
        input_gradient, normalized_rows, dhid, zlow, dbias = jax.vmap(one_history, in_axes=(0, 0, 0, 0, None, None, None))(history_in, upstream, lens, times, w_in, w_out, time_bias)
        normed_c = normalized_rows.astype(jnp.float32).reshape(SEQ_DEV, N_CTX, S_DEV, D)
        dhid_c = dhid.astype(jnp.float32).reshape(SEQ_DEV, N_CTX, S_DEV, 4 * H * DH)
        zlow_c = zlow.astype(jnp.float32).reshape(SEQ_DEV, N_CTX, S_DEV, H * DH)
        up_c = upstream.astype(jnp.float32).reshape(SEQ_DEV, N_CTX, S_DEV, D)
        acc_in = acc_in + rounded_sum(jnp.einsum('scim,scin->cmn', normed_c, dhid_c))
        acc_out = acc_out + rounded_sum(jnp.einsum('scim,scin->cmn', zlow_c, up_c))
        acc_bias = acc_bias + lax.optimization_barrier(jnp.sum(dbias, axis=0))
        return ((acc_in, acc_out, acc_bias), input_gradient)
    start = (jnp.zeros((D, 4 * H * DH), jnp.float32), jnp.zeros((H * DH, D), jnp.float32), jnp.zeros((H, NB), jnp.float32))
    sums, grads = lax.scan(group_step, start, jnp.arange(groups, dtype=jnp.int32))
    input_gradient = grads.reshape(NSEQ, L, D)
    return (input_gradient, sums[0] / NSEQ, sums[1] / NSEQ, sums[2] / NSEQ)
```

```python
import functools

import jax
import jax.numpy as jnp
from jax import lax
from jax.experimental import pallas as pl
from jax.experimental.pallas import tpu as pltpu
from jax.sharding import Mesh
from jax.sharding import PartitionSpec as P

DH = 256
D = 1024
L = 1024
EPS = 1e-05
BF = jnp.bfloat16
F32 = jnp.float32
BQ = 256
NQ = L // BQ
SHARD = 176
PLANE = ("yh", "core", "yl", "x")
CHIPS = ("yh", "yl", "x")
ANY = pl.BlockSpec(memory_space=pl.ANY)
VM = pl.BlockSpec(memory_space=pltpu.VMEM)
SM = pl.BlockSpec(memory_space=pltpu.SMEM)


def params(mib):
    return pltpu.CompilerParams(vmem_limit_bytes=mib << 20)


def shape(dims, kind):
    return jax.ShapeDtypeStruct(dims, kind)


def nn(a, b):
    return lax.dot_general(a, b, (((1,), (0,)), ((), ())), preferred_element_type=F32)


def nt(a, b):
    return lax.dot_general(a, b, (((1,), (1,)), ((), ())), preferred_element_type=F32)


def tn(a, b):
    return lax.dot_general(a, b, (((0,), (0,)), ((), ())), preferred_element_type=F32)


def rows(start, size):
    return pl.ds(pl.multiple_of(start, size), size)


def run_copies(copies):
    for c in copies:
        c.start()
    for c in copies:
        c.wait()


def select_kernel(meta, lay, grad, small, *refs):
    outs, sem = refs[:8], refs[8]
    copies = []
    for k in range(4):
        copies.append(pltpu.make_async_copy(lay.at[meta[k]], outs[k], sem.at[3 * k]))
        other = meta[4 + k]
        copies.append(
            pltpu.make_async_copy(grad.at[other], outs[4 + k].at[pl.ds(0, 128)], sem.at[3 * k + 1])
        )
        copies.append(
            pltpu.make_async_copy(
                small.at[other], outs[4 + k].at[pl.ds(128, 16)], sem.at[3 * k + 2]
            )
        )
    run_copies(copies)


def select_chunks(meta, lay, grad, small):
    return pl.pallas_call(
        select_kernel,
        out_shape=[shape((128, D), BF)] * 4 + [shape((144, D), BF)] * 4,
        in_specs=[SM, ANY, ANY, ANY],
        out_specs=[ANY] * 8,
        scratch_shapes=[pltpu.SemaphoreType.DMA((12,))],
        name="select_chunks",
    )(meta, lay, grad, small)


def load_weights(wag, w, sem, first):
    return [
        pltpu.make_async_copy(
            wag.at[pl.ds(160 * z, 128)], w.at[pl.ds(128 * z, 128)], sem.at[first + z]
        )
        for z in range(8)
    ]


def forward_kernel(meta, tb, *refs):
    xs, gs = refs[:8], refs[8:16]
    wag, wrecv = refs[16:18]
    normed, act, slope, probs, pslope, mixed, dz, stats, grad, srow = refs[18:28]
    x, w, wo, small, scol, sem = refs[28:]
    e, p, h = meta[0], meta[1], meta[2]
    copies = load_weights(wag, w, sem, 0)
    for k in range(8):
        half = h if k < 4 else 1 - h
        bx = half * 4 + jnp.bitwise_xor(e, k % 4)
        bg = half * 4 + jnp.bitwise_xor(p, k % 4)
        copies.append(pltpu.make_async_copy(xs[k], x.at[rows(bx * 128, 128)], sem.at[8 + k]))
        copies.append(
            pltpu.make_async_copy(
                gs[k].at[pl.ds(0, 128)], grad.at[rows(bg * 128, 128)], sem.at[16 + k]
            )
        )
        copies.append(
            pltpu.make_async_copy(
                gs[k].at[pl.ds(128, 16), pl.ds(0, 128)], small.at[bg], sem.at[24 + k]
            )
        )
    for q in range(4):
        for r in range(2):
            own = wag.at[
                pl.ds(pl.multiple_of((4 * h + q) * 160 + 128, 32), 32), pl.ds(512 * r, 512)
            ]
            other = wrecv.at[q, :, pl.ds(512 * r, 512)]
            to = pl.ds(64 * q + 32 * r, 32)
            copies.append(
                pltpu.make_async_copy(own, wo.at[to, rows(h * 512, 512)], sem.at[32 + 4 * q + r])
            )
            copies.append(
                pltpu.make_async_copy(
                    other, wo.at[to, rows((1 - h) * 512, 512)], sem.at[34 + 4 * q + r]
                )
            )
    run_copies(copies)

    def project(i, carry):
        at = rows(i * BQ, BQ)
        v = x[at, :].astype(F32)
        v = v - jnp.mean(v, axis=-1, keepdims=True)
        r = lax.rsqrt(jnp.mean(v * v, axis=-1, keepdims=True) + EPS)
        n = (v * r).astype(BF)
        normed[at, :] = n
        stats[at, :] = jnp.broadcast_to(r, (BQ, 128))
        for c in range(4):
            cols = pl.ds(256 * c, 256)
            hidden = nn(n, w[:, cols])
            sg = jax.nn.sigmoid(hidden)
            act[at, cols] = (hidden * sg).astype(BF)
            slope[at, cols] = (sg * (1.0 + hidden * (1.0 - sg))).astype(BF)
        return carry

    lax.fori_loop(0, NQ, project, 0)

    for b in range(8):
        tile = small[b].astype(F32)
        srow[0:8, pl.ds(128 * b, 128)] = tile[0:8]
        full = jnp.concatenate([tile, jnp.zeros((112, 128), F32)], axis=0)
        scol[pl.ds(128 * b, 128), :] = jnp.transpose(full)

    table = jnp.broadcast_to(tb[0:1, :], (BQ, 128))
    lane = lax.broadcasted_iota(jnp.int32, (BQ, 128), 1)
    causal = (
        lax.broadcasted_iota(jnp.int32, (BQ, BQ), 1)
        <= lax.broadcasted_iota(jnp.int32, (BQ, BQ), 0)
    )
    for i in range(NQ):
        at = pl.ds(i * BQ, BQ)
        q = (act[at, 512:768].astype(F32) * (DH**-0.5)).astype(BF)
        si = scol[at, 0:1]
        lv = scol[at, 1:2]
        for j in range(i + 1):
            cols = pl.ds(j * BQ, BQ)
            s = nt(q, act[cols, 768:1024])
            near = jnp.clip(si - srow[0:1, cols], 0.0, 127.0).astype(jnp.int32)
            bias = jnp.concatenate(
                [
                    jnp.take_along_axis(table, near[:, :128], axis=1, mode="promise_in_bounds"),
                    jnp.take_along_axis(table, near[:, 128:], axis=1, mode="promise_in_bounds"),
                ],
                axis=1,
            )
            s = s + bias
            sg = jax.nn.sigmoid(s)
            live = jnp.where(causal, lv, 0.0) if j == i else lv
            sg = sg * 1.0
            probs[at, cols] = (s * sg * live).astype(BF)
            pslope[at, cols] = (sg * (1.0 + s * (1.0 - sg)) * live).astype(BF)
        upto = (i + 1) * BQ
        mix = nn(probs[at, 0:upto], act[0:upto, 256:512])
        mixed[at, :] = mix
        d = nt(grad[at, :], wo[...])
        dz[at, :] = d
        gated = mix * act[at, 0:256].astype(F32)
        m = jnp.mean(gated, axis=-1, keepdims=True)
        centred = gated - m
        m2 = jnp.sum(centred * centred, axis=-1, keepdims=True)
        s3 = jnp.sum(d, axis=-1, keepdims=True)
        s4 = jnp.sum(d * centred, axis=-1, keepdims=True)
        row = stats[at, :]
        for n, value in enumerate((m, m2, s3, s4)):
            row = jnp.where(lane == n, value, row)
        row = jnp.where(lane == 5, si, row)
        stats[at, :] = row


def forward(meta, tb, xs, gs, wag, wrecv):
    return pl.pallas_call(
        forward_kernel,
        out_shape=[
            shape((L, D), BF),
            shape((L, D), BF),
            shape((L, D), BF),
            shape((L, L), BF),
            shape((L, L), BF),
            shape((L, DH), F32),
            shape((L, DH), F32),
            shape((L, 128), F32),
            shape((L, D), BF),
            shape((8, L), F32),
        ],
        in_specs=[SM, VM] + [ANY] * 18,
        out_specs=[VM] * 10,
        scratch_shapes=[
            pltpu.VMEM((L, D), BF),
            pltpu.VMEM((D, D), BF),
            pltpu.VMEM((DH, D), BF),
            pltpu.VMEM((8, 16, 128), BF),
            pltpu.VMEM((L, 128), F32),
            pltpu.SemaphoreType.DMA((48,)),
        ],
        compiler_params=params(48),
        name="forward",
    )(meta, tb, *xs, *gs, wag, wrecv)


def middle_kernel(meta, own, peer, mixed, dz, gate, gslope, grad, datt, dhu, keep, send, zl):
    h = meta[2]

    def step(i, carry):
        at = rows(i * BQ, BQ)
        a, b = own[at, :], peer[at, :]
        m0, m1 = a[:, 0:1], b[:, 0:1]
        mean = 0.5 * (m0 + m1)
        gap = m0 - mean
        r = lax.rsqrt((a[:, 1:2] + b[:, 1:2] + 512.0 * gap * gap) * (1.0 / 512.0) + EPS)
        dmean = (a[:, 2:3] + b[:, 2:3]) * (1.0 / 512.0)
        cross = a[:, 3:4] + b[:, 3:4] + gap * (a[:, 2:3] - b[:, 2:3])
        cross = cross * r * (1.0 / 512.0)
        mix = mixed[at, :]
        u = gate[at, :].astype(F32)
        zhat = (mix * u - mean) * r
        zl[at, :] = zhat.astype(BF)
        dgated = r * (dz[at, :] - dmean - zhat * cross)
        datt[at, :] = (dgated * u).astype(BF)
        dhu[at, :] = (dgated * mix * gslope[at, :].astype(F32)).astype(BF)
        return carry

    lax.fori_loop(0, NQ, step, 0)
    for half in range(2):
        po = tn(zl[...], grad[:, 512 * half : 512 * half + 512]).astype(BF)
        for q in range(4):
            block = jnp.concatenate(
                [po[64 * q : 64 * q + 32], po[64 * q + 32 : 64 * q + 64]], axis=1
            )

            @pl.when(h == half)
            def _(block=block, q=q):
                keep[q] = block

            @pl.when(h != half)
            def _(block=block, q=q):
                send[q] = block


def middle(meta, own, peer, mixed, dz, act, slope, grad):
    first = pl.BlockSpec((L, DH), lambda i: (0, 0))

    def whole(*dims):
        return pl.BlockSpec(dims, lambda i: (0,) * len(dims))

    return pl.pallas_call(
        middle_kernel,
        grid=(1,),
        out_shape=[
            shape((L, DH), BF),
            shape((L, DH), BF),
            shape((4, 32, D), BF),
            shape((4, 32, D), BF),
        ],
        in_specs=[SM, whole(L, 128), whole(L, 128), whole(L, DH), whole(L, DH), first, first, whole(L, D)],
        out_specs=[whole(L, DH), whole(L, DH), whole(4, 32, D), whole(4, 32, D)],
        scratch_shapes=[pltpu.VMEM((L, DH), BF)],
        compiler_params=params(48),
        name="middle",
    )(meta, own, peer, mixed, dz, act, slope, grad)


def backward_kernel(
    meta, act, slope, probs, pslope, datt, dhu, normed, stats, keep, recv, part, dhid, dlow, hot
):
    h = meta[2]
    stamp_lane = lax.broadcasted_iota(jnp.int32, (L, 256), 1).astype(F32)
    hot[...] = jnp.where(stats[:, 5:6] == stamp_lane, 1.0, 0.0).astype(BF)
    dhid[:, 0:256] = dhu[...]
    bucket = lax.broadcasted_iota(jnp.int32, (BQ, 128), 1)
    time = lax.broadcasted_iota(jnp.int32, (BQ, 256), 1)
    total = jnp.zeros((BQ, 128), F32)
    for i in range(NQ):
        at = pl.ds(i * BQ, BQ)
        upto = (i + 1) * BQ
        da = datt[at, :]
        for j in range(i + 1):
            cols = pl.ds(j * BQ, BQ)
            dp = nt(da, act[cols, 256:512])
            dlow[at, cols] = (dp * pslope[at, cols].astype(F32)).astype(BF)
        low = dlow[at, 0:upto]
        dq = nn(low, act[0:upto, 768:1024]) * (DH**-0.5)
        dhid[at, 512:768] = (dq * slope[at, 512:768].astype(F32)).astype(BF)
        by_time = nn(low, hot[0:upto, :])
        si = stats[at, 5:6].astype(jnp.int32)
        when = si - bucket
        index = jnp.bitwise_and(when, 127)
        early = jnp.take_along_axis(by_time[:, :128], index, axis=1, mode="promise_in_bounds")
        late = jnp.take_along_axis(by_time[:, 128:], index, axis=1, mode="promise_in_bounds")
        picked = jnp.where(when >= 128, late, jnp.where(when >= 0, early, 0.0))
        far = jnp.sum(jnp.where(time <= si - 127, by_time, 0.0), axis=-1, keepdims=True)
        total = total + jnp.where(bucket == 127, far, picked)
    for j in range(NQ):
        cols = pl.ds(j * BQ, BQ)
        frm = j * BQ
        dv = tn(probs[frm:, cols], datt[frm:, :])
        dhid[cols, 256:512] = (dv * slope[cols, 256:512].astype(F32)).astype(BF)
        dk = tn(dlow[frm:, cols], act[frm:, 512:768]) * (DH**-0.5)
        dhid[cols, 768:1024] = (dk * slope[cols, 768:1024].astype(F32)).astype(BF)
    for b in range(4):
        for c in range(4):
            cols = pl.ds(256 * c, 256)
            pin = tn(normed[:, 256 * b : 256 * b + 256], dhid[:, cols]).astype(BF)
            part[pl.ds(2 * b * SHARD, 128), cols] = pin[:128]
            part[pl.ds((2 * b + 1) * SHARD, 128), cols] = pin[128:]
    bias = jnp.sum(total, axis=0, keepdims=True)
    high = bias.astype(BF)
    low = (bias - high.astype(F32)).astype(BF)
    line = jnp.concatenate([high.astype(F32), low.astype(F32), jnp.zeros((1, 768), F32)], axis=1)
    line = jnp.where(
        lax.broadcasted_iota(jnp.int32, (16, D), 0) == 0, jnp.broadcast_to(line, (16, D)), 0.0
    ).astype(BF)
    for z in range(8):
        part[pl.ds(z * SHARD + 160, 16), :] = line
    for q in range(4):
        part[pl.ds(pl.multiple_of((4 * h + q) * SHARD + 128, 16), 32), :] = keep[q]
        part[pl.ds(pl.multiple_of((4 * (1 - h) + q) * SHARD + 128, 16), 32), :] = recv[q]


def backward(meta, act, slope, probs, pslope, datt, dhu, normed, stats, keep, recv):
    return pl.pallas_call(
        backward_kernel,
        out_shape=[shape((8 * SHARD, D), BF), shape((L, D), BF)],
        in_specs=[SM] + [VM] * 10,
        out_specs=[VM, VM],
        scratch_shapes=[pltpu.VMEM((L, L), BF), pltpu.VMEM((L, 256), BF)],
        compiler_params=params(48),
        name="backward",
    )(meta, act, slope, probs, pslope, datt, dhu, normed, stats, keep, recv)


def input_kernel(meta, dhid, normed, stats, wag, own, other, w, sem):
    h = meta[2]
    run_copies(load_weights(wag, w, sem, 0))
    for i in range(NQ):
        at = pl.ds(i * BQ, BQ)
        dn = nt(dhid[at, :], w[...])
        n = normed[at, :].astype(F32)
        r = stats[at, 4:5]
        mean = jnp.mean(dn, axis=-1, keepdims=True)
        cross = jnp.mean(dn * n, axis=-1, keepdims=True)
        res = (r * (dn - mean - n * cross)).astype(BF)
        to = pl.ds((i % 2) * BQ, BQ)

        @pl.when(h == i // 2)
        def _(res=res, to=to):
            own[to, :] = res

        @pl.when(h != i // 2)
        def _(res=res, to=to):
            other[to, :] = res


def input_grad(meta, dhid, normed, stats, wag):
    return pl.pallas_call(
        input_kernel,
        out_shape=[shape((512, D), BF)] * 2,
        in_specs=[SM] + [VM] * 3 + [ANY],
        out_specs=[VM, VM],
        scratch_shapes=[pltpu.VMEM((D, D), BF), pltpu.SemaphoreType.DMA((8,))],
        compiler_params=params(48),
        name="input_grad",
    )(meta, dhid, normed, stats, wag)


def add_kernel(meta, a, b, *outs):
    p = meta[1]
    for k in range(4):
        at = rows(jnp.bitwise_xor(p, k) * 128, 128)
        outs[k][...] = (a[at, :].astype(F32) + b[at, :].astype(F32)).astype(BF)


def add_halves(meta, a, b):
    return pl.pallas_call(
        add_kernel,
        out_shape=[shape((128, D), BF)] * 4,
        in_specs=[SM, VM, VM],
        out_specs=[VM] * 4,
        compiler_params=params(32),
        name="add_halves",
    )(meta, a, b)


def place_kernel(meta, *refs):
    chunks, out, sem = refs[:4], refs[4], refs[5]
    run_copies(
        [
            pltpu.make_async_copy(chunks[k], out.at[jnp.bitwise_xor(meta[3], k)], sem.at[k])
            for k in range(4)
        ]
    )


def place(meta, chunks):
    return pl.pallas_call(
        place_kernel,
        out_shape=shape((4, 128, D), BF),
        in_specs=[SM] + [ANY] * 4,
        out_specs=ANY,
        scratch_shapes=[pltpu.SemaphoreType.DMA((4,))],
        name="place",
    )(meta, *chunks)


def device(yh, core, yl, x):
    return ((yh * 2 + core) * 2 + yl) * 4 + x


def unit_device(e, p, half):
    ye, ce = e >> 1, e & 1
    yp, cp = p >> 1, p & 1
    return device(ye, half, yp, 2 * (ye ^ cp) + ce)


def input_pairs(k):
    pairs = []
    for p in range(4):
        for yl in range(2):
            for x in range(4):
                pairs.append((device(p >> 1, p & 1, yl, x), unit_device(x ^ k, p, yl)))
    return pairs


def grad_pairs(k):
    pairs = []
    for e in range(4):
        for yl in range(2):
            for x in range(4):
                pairs.append((device(e >> 1, e & 1, yl, x), unit_device(e, x ^ k, yl)))
    return pairs


def back_pairs(k):
    return [(b, a) for a, b in grad_pairs(k)]


def local(layer_in, repack_plan, lengths, stamps, w_in, w_out, time_bias, grad_out):
    yh, core, yl, x = (lax.axis_index(n).astype(jnp.int32) for n in PLANE)
    swap = functools.partial(lax.ppermute, axis_name="core", perm=[(0, 1), (1, 0)])
    first = core == 0
    unit_e = 2 * yh + jnp.bitwise_and(x, 1)
    unit_p = 2 * yl + jnp.bitwise_xor(lax.shift_right_logical(x, 1), yh)
    meta = jnp.stack([unit_e, unit_p, core, x])

    w5 = w_in.reshape(128, 4, 2, DH)
    w_half = jnp.where(first, w5[:, :, 0], w5[:, :, 1]).reshape(128, D)
    o_half = jnp.where(first, w_out[:, :512], w_out[:, 512:])
    o_half = jnp.concatenate([o_half[:32], o_half[32:]], axis=1)
    wag = lax.all_gather(jnp.concatenate([w_half, o_half], axis=0), "z", axis=0, tiled=True)
    w3 = wag.reshape(8, 160, D)
    wrecv = swap(jnp.where(first, w3[4:, 128:], w3[:4, 128:]))

    here = (yl * 4 + x) * 128 + lax.iota(jnp.int32, 128)
    alive = here[None, :] < lengths[:, None]
    small = jnp.stack([stamps.astype(BF), alive.astype(BF)], axis=1)
    small = jnp.pad(small, ((0, 0), (0, 14), (0, D - 128)))
    others = [jnp.bitwise_xor(x, k) for k in range(4)]
    slots = [
        sum(jnp.where(o == t, repack_plan[t], 0) for t in range(4)).astype(jnp.int32)
        for o in others
    ]
    chunks = select_chunks(jnp.stack(slots + others), layer_in, grad_out, small)
    xs = [lax.ppermute(chunks[k], PLANE, input_pairs(k)) for k in range(4)]
    gs = [lax.ppermute(chunks[4 + k], PLANE, grad_pairs(k)) for k in range(4)]
    xs = xs + [swap(c) for c in xs]
    gs = gs + [swap(c) for c in gs]
    tb = jnp.where(first, time_bias[0:1], time_bias[1:2]).astype(F32)

    normed, act, slope, probs, pslope, mixed, dz, stats, grad, _ = forward(
        meta, tb, xs, gs, wag, wrecv
    )
    datt, dhu, keep, send = middle(meta, stats, swap(stats), mixed, dz, act, slope, grad)
    part, dhid = backward(
        meta, act, slope, probs, pslope, datt, dhu, normed, stats, keep, swap(send)
    )
    mine = lax.psum_scatter(part, "z", scatter_dimension=0, tiled=True)
    own, other = input_grad(meta, dhid, normed, stats, wag)
    pieces = add_halves(meta, own, swap(other))
    back = [lax.ppermute(pieces[k], PLANE, back_pairs(k)) for k in range(4)]
    input_gradient = place(meta, back)

    def exchange(v):
        return lax.all_to_all(v, CHIPS, split_axis=0, concat_axis=0, tiled=True)

    spread = exchange(mine.reshape(16, SHARD // 16, D))
    summed = jnp.sum(spread.astype(F32), axis=0, keepdims=True).astype(BF)
    mine = exchange(jnp.broadcast_to(summed, (16, SHARD // 16, D))).reshape(SHARD, D)
    theirs = swap(mine)
    pair0 = jnp.where(first, mine, theirs).astype(F32) * (1.0 / 128.0)
    pair1 = jnp.where(first, theirs, mine).astype(F32) * (1.0 / 128.0)
    grad_w_in = jnp.stack(
        [pair0[:128].reshape(128, 4, DH), pair1[:128].reshape(128, 4, DH)], axis=2
    ).reshape(128, 2 * D)

    def unfold(v):
        return jnp.concatenate([v[128:160, :512], v[128:160, 512:]], axis=0)

    grad_w_out = jnp.concatenate([unfold(pair0), unfold(pair1)], axis=1)
    grad_bias = jnp.stack([v[160, :128] + v[160, 128:256] for v in (pair0, pair1)])
    return input_gradient, grad_w_in, grad_w_out, grad_bias


def solution(mesh):
    fine = Mesh(mesh.devices.reshape(2, 2, 2, 4, 8), ("yh", "core", "yl", "x", "z"))
    events = P(("yh", "core", "z"), ("yl", "x"), None)
    slots = P(("yh", "core", "z"))
    return jax.shard_map(
        local,
        mesh=fine,
        in_specs=(
            events,
            slots,
            slots,
            P(("yh", "core", "z"), ("yl", "x")),
            P("z", None),
            P("z", None),
            P(),
            events,
        ),
        out_specs=(events, P("z", None), P("z", None), P()),
        check_vma=False,
    )
```

```python
import functools

import jax
import jax.numpy as jnp
from jax import lax
from jax.experimental import pallas as pl
from jax.experimental.pallas import tpu as pltpu
from jax.sharding import Mesh
from jax.sharding import PartitionSpec as P

DH = 256
D = 1024
L = 1024
EPS = 1e-05
BF = jnp.bfloat16
F32 = jnp.float32
BQ = 256
NQ = L // BQ
SHARD = 176
PLANE = ("yh", "core", "yl", "x")
CHIPS = ("yh", "yl", "x")
ANY = pl.BlockSpec(memory_space=pl.ANY)
VM = pl.BlockSpec(memory_space=pltpu.VMEM)
SM = pl.BlockSpec(memory_space=pltpu.SMEM)


def params(mib):
    return pltpu.CompilerParams(vmem_limit_bytes=mib << 20)


def shape(dims, kind):
    return jax.ShapeDtypeStruct(dims, kind)


def nn(a, b):
    return lax.dot_general(a, b, (((1,), (0,)), ((), ())), preferred_element_type=F32)


def nt(a, b):
    return lax.dot_general(a, b, (((1,), (1,)), ((), ())), preferred_element_type=F32)


def tn(a, b):
    return lax.dot_general(a, b, (((0,), (0,)), ((), ())), preferred_element_type=F32)


def rows(start, size):
    return pl.ds(pl.multiple_of(start, size), size)


def run_copies(copies):
    for c in copies:
        c.start()
    for c in copies:
        c.wait()


def select_kernel(meta, lay, grad, small, *refs):
    outs, sem = refs[:8], refs[8]
    copies = []
    for k in range(4):
        copies.append(pltpu.make_async_copy(lay.at[meta[k]], outs[k], sem.at[3 * k]))
        other = meta[4 + k]
        copies.append(
            pltpu.make_async_copy(grad.at[other], outs[4 + k].at[pl.ds(0, 128)], sem.at[3 * k + 1])
        )
        copies.append(
            pltpu.make_async_copy(
                small.at[other], outs[4 + k].at[pl.ds(128, 16)], sem.at[3 * k + 2]
            )
        )
    run_copies(copies)


def select_chunks(meta, lay, grad, small):
    return pl.pallas_call(
        select_kernel,
        out_shape=[shape((128, D), BF)] * 4 + [shape((144, D), BF)] * 4,
        in_specs=[SM, ANY, ANY, ANY],
        out_specs=[VM] * 8,
        scratch_shapes=[pltpu.SemaphoreType.DMA((12,))],
        compiler_params=params(32),
        name="select_chunks",
    )(meta, lay, grad, small)


def load_weights(wag, w, sem, first):
    return [
        pltpu.make_async_copy(
            wag.at[pl.ds(160 * z, 128)], w.at[pl.ds(128 * z, 128)], sem.at[first + z]
        )
        for z in range(8)
    ]


def forward_kernel(meta, tb, *refs):
    xs, gs = refs[:8], refs[8:16]
    wag, wrecv = refs[16:18]
    normed, act, slope, probs, pslope, mixed, dz, stats, grad, srow = refs[18:28]
    x, w, wo, small, scol, sem = refs[28:]
    e, p, h = meta[0], meta[1], meta[2]
    copies = load_weights(wag, w, sem, 0)
    for k in range(8):
        half = h if k < 4 else 1 - h
        bx = half * 4 + jnp.bitwise_xor(e, k % 4)
        bg = half * 4 + jnp.bitwise_xor(p, k % 4)
        copies.append(pltpu.make_async_copy(xs[k], x.at[rows(bx * 128, 128)], sem.at[8 + k]))
        copies.append(
            pltpu.make_async_copy(
                gs[k].at[pl.ds(0, 128)], grad.at[rows(bg * 128, 128)], sem.at[16 + k]
            )
        )
        copies.append(
            pltpu.make_async_copy(
                gs[k].at[pl.ds(128, 16), pl.ds(0, 128)], small.at[bg], sem.at[24 + k]
            )
        )
    for q in range(4):
        for r in range(2):
            own = wag.at[
                pl.ds(pl.multiple_of((4 * h + q) * 160 + 128, 32), 32), pl.ds(512 * r, 512)
            ]
            other = wrecv.at[q, :, pl.ds(512 * r, 512)]
            to = pl.ds(64 * q + 32 * r, 32)
            copies.append(
                pltpu.make_async_copy(own, wo.at[to, rows(h * 512, 512)], sem.at[32 + 4 * q + r])
            )
            copies.append(
                pltpu.make_async_copy(
                    other, wo.at[to, rows((1 - h) * 512, 512)], sem.at[34 + 4 * q + r]
                )
            )
    run_copies(copies)

    def project(i, carry):
        at = rows(i * BQ, BQ)
        v = x[at, :].astype(F32)
        v = v - jnp.mean(v, axis=-1, keepdims=True)
        r = lax.rsqrt(jnp.mean(v * v, axis=-1, keepdims=True) + EPS)
        n = (v * r).astype(BF)
        normed[at, :] = n
        stats[at, :] = jnp.broadcast_to(r, (BQ, 128))
        for c in range(4):
            cols = pl.ds(256 * c, 256)
            hidden = nn(n, w[:, cols])
            sg = jax.nn.sigmoid(hidden)
            act[at, cols] = (hidden * sg).astype(BF)
            slope[at, cols] = (sg * (1.0 + hidden * (1.0 - sg))).astype(BF)
        return carry

    lax.fori_loop(0, NQ, project, 0)

    for b in range(8):
        tile = small[b].astype(F32)
        srow[0:8, pl.ds(128 * b, 128)] = tile[0:8]
        full = jnp.concatenate([tile, jnp.zeros((112, 128), F32)], axis=0)
        scol[pl.ds(128 * b, 128), :] = jnp.transpose(full)

    table = jnp.broadcast_to(tb[0:1, :], (BQ, 128))
    lane = lax.broadcasted_iota(jnp.int32, (BQ, 128), 1)
    causal = (
        lax.broadcasted_iota(jnp.int32, (BQ, BQ), 1)
        <= lax.broadcasted_iota(jnp.int32, (BQ, BQ), 0)
    )
    for i in range(NQ):
        at = pl.ds(i * BQ, BQ)
        q = (act[at, 512:768].astype(F32) * (DH**-0.5)).astype(BF)
        si = scol[at, 0:1]
        lv = scol[at, 1:2]
        for j in range(i + 1):
            cols = pl.ds(j * BQ, BQ)
            s = nt(q, act[cols, 768:1024])
            near = jnp.clip(si - srow[0:1, cols], 0.0, 127.0).astype(jnp.int32)
            bias = jnp.concatenate(
                [
                    jnp.take_along_axis(table, near[:, :128], axis=1, mode="promise_in_bounds"),
                    jnp.take_along_axis(table, near[:, 128:], axis=1, mode="promise_in_bounds"),
                ],
                axis=1,
            )
            s = s + bias
            sg = jax.nn.sigmoid(s)
            live = jnp.where(causal, lv, 0.0) if j == i else lv
            sg = sg * 1.0
            probs[at, cols] = (s * sg * live).astype(BF)
            pslope[at, cols] = (sg * (1.0 + s * (1.0 - sg)) * live).astype(BF)
        upto = (i + 1) * BQ
        mix = nn(probs[at, 0:upto], act[0:upto, 256:512])
        mixed[at, :] = mix
        d = nt(grad[at, :], wo[...])
        dz[at, :] = d
        gated = mix * act[at, 0:256].astype(F32)
        m = jnp.mean(gated, axis=-1, keepdims=True)
        centred = gated - m
        m2 = jnp.sum(centred * centred, axis=-1, keepdims=True)
        s3 = jnp.sum(d, axis=-1, keepdims=True)
        s4 = jnp.sum(d * centred, axis=-1, keepdims=True)
        row = stats[at, :]
        for n, value in enumerate((m, m2, s3, s4)):
            row = jnp.where(lane == n, value, row)
        row = jnp.where(lane == 5, si, row)
        stats[at, :] = row


def forward(meta, tb, xs, gs, wag, wrecv):
    return pl.pallas_call(
        forward_kernel,
        out_shape=[
            shape((L, D), BF),
            shape((L, D), BF),
            shape((L, D), BF),
            shape((L, L), BF),
            shape((L, L), BF),
            shape((L, DH), F32),
            shape((L, DH), F32),
            shape((L, 128), F32),
            shape((L, D), BF),
            shape((8, L), F32),
        ],
        in_specs=[SM, VM] + [ANY] * 18,
        out_specs=[VM] * 10,
        scratch_shapes=[
            pltpu.VMEM((L, D), BF),
            pltpu.VMEM((D, D), BF),
            pltpu.VMEM((DH, D), BF),
            pltpu.VMEM((8, 16, 128), BF),
            pltpu.VMEM((L, 128), F32),
            pltpu.SemaphoreType.DMA((48,)),
        ],
        compiler_params=params(48),
        name="forward",
    )(meta, tb, *xs, *gs, wag, wrecv)


def middle_kernel(meta, own, peer, mixed, dz, gate, gslope, grad, datt, dhu, keep, send, zl):
    h = meta[2]

    def step(i, carry):
        at = rows(i * BQ, BQ)
        a, b = own[at, :], peer[at, :]
        m0, m1 = a[:, 0:1], b[:, 0:1]
        mean = 0.5 * (m0 + m1)
        gap = m0 - mean
        r = lax.rsqrt((a[:, 1:2] + b[:, 1:2] + 512.0 * gap * gap) * (1.0 / 512.0) + EPS)
        dmean = (a[:, 2:3] + b[:, 2:3]) * (1.0 / 512.0)
        cross = a[:, 3:4] + b[:, 3:4] + gap * (a[:, 2:3] - b[:, 2:3])
        cross = cross * r * (1.0 / 512.0)
        mix = mixed[at, :]
        u = gate[at, :].astype(F32)
        zhat = (mix * u - mean) * r
        zl[at, :] = zhat.astype(BF)
        dgated = r * (dz[at, :] - dmean - zhat * cross)
        datt[at, :] = (dgated * u).astype(BF)
        dhu[at, :] = (dgated * mix * gslope[at, :].astype(F32)).astype(BF)
        return carry

    lax.fori_loop(0, NQ, step, 0)
    for half in range(2):
        po = tn(zl[...], grad[:, 512 * half : 512 * half + 512]).astype(BF)
        for q in range(4):
            block = jnp.concatenate(
                [po[64 * q : 64 * q + 32], po[64 * q + 32 : 64 * q + 64]], axis=1
            )

            @pl.when(h == half)
            def _(block=block, q=q):
                keep[q] = block

            @pl.when(h != half)
            def _(block=block, q=q):
                send[q] = block


def middle(meta, own, peer, mixed, dz, act, slope, grad):
    first = pl.BlockSpec((L, DH), lambda i: (0, 0))

    def whole(*dims):
        return pl.BlockSpec(dims, lambda i: (0,) * len(dims))

    return pl.pallas_call(
        middle_kernel,
        grid=(1,),
        out_shape=[
            shape((L, DH), BF),
            shape((L, DH), BF),
            shape((4, 32, D), BF),
            shape((4, 32, D), BF),
        ],
        in_specs=[SM, whole(L, 128), whole(L, 128), whole(L, DH), whole(L, DH), first, first, whole(L, D)],
        out_specs=[whole(L, DH), whole(L, DH), whole(4, 32, D), whole(4, 32, D)],
        scratch_shapes=[pltpu.VMEM((L, DH), BF)],
        compiler_params=params(48),
        name="middle",
    )(meta, own, peer, mixed, dz, act, slope, grad)


def backward_kernel(
    meta, act, slope, probs, pslope, datt, dhu, normed, stats, keep, recv, part, dhid, dlow, hot
):
    h = meta[2]
    stamp_lane = lax.broadcasted_iota(jnp.int32, (L, 256), 1).astype(F32)
    hot[...] = jnp.where(stats[:, 5:6] == stamp_lane, 1.0, 0.0).astype(BF)
    dhid[:, 0:256] = dhu[...]
    bucket = lax.broadcasted_iota(jnp.int32, (BQ, 128), 1)
    time = lax.broadcasted_iota(jnp.int32, (BQ, 256), 1)
    total = jnp.zeros((BQ, 128), F32)
    for i in range(NQ):
        at = pl.ds(i * BQ, BQ)
        upto = (i + 1) * BQ
        da = datt[at, :]
        for j in range(i + 1):
            cols = pl.ds(j * BQ, BQ)
            dp = nt(da, act[cols, 256:512])
            dlow[at, cols] = (dp * pslope[at, cols].astype(F32)).astype(BF)
        low = dlow[at, 0:upto]
        dq = nn(low, act[0:upto, 768:1024]) * (DH**-0.5)
        dhid[at, 512:768] = (dq * slope[at, 512:768].astype(F32)).astype(BF)
        by_time = nn(low, hot[0:upto, :])
        si = stats[at, 5:6].astype(jnp.int32)
        when = si - bucket
        index = jnp.bitwise_and(when, 127)
        early = jnp.take_along_axis(by_time[:, :128], index, axis=1, mode="promise_in_bounds")
        late = jnp.take_along_axis(by_time[:, 128:], index, axis=1, mode="promise_in_bounds")
        picked = jnp.where(when >= 128, late, jnp.where(when >= 0, early, 0.0))
        far = jnp.sum(jnp.where(time <= si - 127, by_time, 0.0), axis=-1, keepdims=True)
        total = total + jnp.where(bucket == 127, far, picked)
    for j in range(NQ):
        cols = pl.ds(j * BQ, BQ)
        frm = j * BQ
        dv = tn(probs[frm:, cols], datt[frm:, :])
        dhid[cols, 256:512] = (dv * slope[cols, 256:512].astype(F32)).astype(BF)
        dk = tn(dlow[frm:, cols], act[frm:, 512:768]) * (DH**-0.5)
        dhid[cols, 768:1024] = (dk * slope[cols, 768:1024].astype(F32)).astype(BF)
    for b in range(4):
        for c in range(4):
            cols = pl.ds(256 * c, 256)
            pin = tn(normed[:, 256 * b : 256 * b + 256], dhid[:, cols]).astype(BF)
            part[pl.ds(2 * b * SHARD, 128), cols] = pin[:128]
            part[pl.ds((2 * b + 1) * SHARD, 128), cols] = pin[128:]
    bias = jnp.sum(total, axis=0, keepdims=True)
    high = bias.astype(BF)
    low = (bias - high.astype(F32)).astype(BF)
    line = jnp.concatenate([high.astype(F32), low.astype(F32), jnp.zeros((1, 768), F32)], axis=1)
    line = jnp.where(
        lax.broadcasted_iota(jnp.int32, (16, D), 0) == 0, jnp.broadcast_to(line, (16, D)), 0.0
    ).astype(BF)
    for z in range(8):
        part[pl.ds(z * SHARD + 160, 16), :] = line
    for q in range(4):
        part[pl.ds(pl.multiple_of((4 * h + q) * SHARD + 128, 16), 32), :] = keep[q]
        part[pl.ds(pl.multiple_of((4 * (1 - h) + q) * SHARD + 128, 16), 32), :] = recv[q]


def backward(meta, act, slope, probs, pslope, datt, dhu, normed, stats, keep, recv):
    return pl.pallas_call(
        backward_kernel,
        out_shape=[shape((8 * SHARD, D), BF), shape((L, D), BF)],
        in_specs=[SM] + [VM] * 10,
        out_specs=[VM, VM],
        scratch_shapes=[pltpu.VMEM((L, L), BF), pltpu.VMEM((L, 256), BF)],
        compiler_params=params(48),
        name="backward",
    )(meta, act, slope, probs, pslope, datt, dhu, normed, stats, keep, recv)


def input_kernel(meta, dhid, normed, stats, wag, own, other, w, sem):
    h = meta[2]
    run_copies(load_weights(wag, w, sem, 0))
    for i in range(NQ):
        at = pl.ds(i * BQ, BQ)
        dn = nt(dhid[at, :], w[...])
        n = normed[at, :].astype(F32)
        r = stats[at, 4:5]
        mean = jnp.mean(dn, axis=-1, keepdims=True)
        cross = jnp.mean(dn * n, axis=-1, keepdims=True)
        res = (r * (dn - mean - n * cross)).astype(BF)
        to = pl.ds((i % 2) * BQ, BQ)

        @pl.when(h == i // 2)
        def _(res=res, to=to):
            own[to, :] = res

        @pl.when(h != i // 2)
        def _(res=res, to=to):
            other[to, :] = res


def input_grad(meta, dhid, normed, stats, wag):
    return pl.pallas_call(
        input_kernel,
        out_shape=[shape((512, D), BF)] * 2,
        in_specs=[SM] + [VM] * 3 + [ANY],
        out_specs=[VM, VM],
        scratch_shapes=[pltpu.VMEM((D, D), BF), pltpu.SemaphoreType.DMA((8,))],
        compiler_params=params(48),
        name="input_grad",
    )(meta, dhid, normed, stats, wag)


def add_kernel(meta, a, b, *outs):
    p = meta[1]
    for k in range(4):
        at = rows(jnp.bitwise_xor(p, k) * 128, 128)
        outs[k][...] = (a[at, :].astype(F32) + b[at, :].astype(F32)).astype(BF)


def add_halves(meta, a, b):
    return pl.pallas_call(
        add_kernel,
        out_shape=[shape((128, D), BF)] * 4,
        in_specs=[SM, VM, VM],
        out_specs=[VM] * 4,
        compiler_params=params(32),
        name="add_halves",
    )(meta, a, b)


def place_kernel(meta, *refs):
    chunks, out, sem = refs[:4], refs[4], refs[5]
    run_copies(
        [
            pltpu.make_async_copy(chunks[k], out.at[jnp.bitwise_xor(meta[3], k)], sem.at[k])
            for k in range(4)
        ]
    )


def place(meta, chunks):
    return pl.pallas_call(
        place_kernel,
        out_shape=shape((4, 128, D), BF),
        in_specs=[SM] + [ANY] * 4,
        out_specs=VM,
        scratch_shapes=[pltpu.SemaphoreType.DMA((4,))],
        compiler_params=params(32),
        name="place",
    )(meta, *chunks)


def device(yh, core, yl, x):
    return ((yh * 2 + core) * 2 + yl) * 4 + x


def unit_device(e, p, half):
    ye, ce = e >> 1, e & 1
    yp, cp = p >> 1, p & 1
    return device(ye, half, yp, 2 * (ye ^ cp) + ce)


def input_pairs(k):
    pairs = []
    for p in range(4):
        for yl in range(2):
            for x in range(4):
                pairs.append((device(p >> 1, p & 1, yl, x), unit_device(x ^ k, p, yl)))
    return pairs


def grad_pairs(k):
    pairs = []
    for e in range(4):
        for yl in range(2):
            for x in range(4):
                pairs.append((device(e >> 1, e & 1, yl, x), unit_device(e, x ^ k, yl)))
    return pairs


def back_pairs(k):
    return [(b, a) for a, b in grad_pairs(k)]


def local(layer_in, repack_plan, lengths, stamps, w_in, w_out, time_bias, grad_out):
    yh, core, yl, x = (lax.axis_index(n).astype(jnp.int32) for n in PLANE)
    swap = functools.partial(lax.ppermute, axis_name="core", perm=[(0, 1), (1, 0)])
    first = core == 0
    unit_e = 2 * yh + jnp.bitwise_and(x, 1)
    unit_p = 2 * yl + jnp.bitwise_xor(lax.shift_right_logical(x, 1), yh)
    meta = jnp.stack([unit_e, unit_p, core, x])

    w5 = w_in.reshape(128, 4, 2, DH)
    w_half = jnp.where(first, w5[:, :, 0], w5[:, :, 1]).reshape(128, D)
    o_half = jnp.where(first, w_out[:, :512], w_out[:, 512:])
    o_half = jnp.concatenate([o_half[:32], o_half[32:]], axis=1)
    wag = lax.all_gather(jnp.concatenate([w_half, o_half], axis=0), "z", axis=0, tiled=True)
    w3 = wag.reshape(8, 160, D)
    wrecv = swap(jnp.where(first, w3[4:, 128:], w3[:4, 128:]))

    here = (yl * 4 + x) * 128 + lax.iota(jnp.int32, 128)
    alive = here[None, :] < lengths[:, None]
    small = jnp.stack([stamps.astype(BF), alive.astype(BF)], axis=1)
    small = jnp.pad(small, ((0, 0), (0, 14), (0, D - 128)))
    others = [jnp.bitwise_xor(x, k) for k in range(4)]
    slots = [
        sum(jnp.where(o == t, repack_plan[t], 0) for t in range(4)).astype(jnp.int32)
        for o in others
    ]
    chunks = select_chunks(jnp.stack(slots + others), layer_in, grad_out, small)
    xs = [lax.ppermute(chunks[k], PLANE, input_pairs(k)) for k in range(4)]
    gs = [lax.ppermute(chunks[4 + k], PLANE, grad_pairs(k)) for k in range(4)]
    xs = xs + [swap(c) for c in xs]
    gs = gs + [swap(c) for c in gs]
    tb = jnp.where(first, time_bias[0:1], time_bias[1:2]).astype(F32)

    normed, act, slope, probs, pslope, mixed, dz, stats, grad, _ = forward(
        meta, tb, xs, gs, wag, wrecv
    )
    datt, dhu, keep, send = middle(meta, stats, swap(stats), mixed, dz, act, slope, grad)
    part, dhid = backward(
        meta, act, slope, probs, pslope, datt, dhu, normed, stats, keep, swap(send)
    )
    mine = lax.psum_scatter(part, "z", scatter_dimension=0, tiled=True)
    own, other = input_grad(meta, dhid, normed, stats, wag)
    pieces = add_halves(meta, own, swap(other))
    back = [lax.ppermute(pieces[k], PLANE, back_pairs(k)) for k in range(4)]
    input_gradient = place(meta, back)
    mine = lax.optimization_barrier((mine, *back))[0]

    def exchange(v):
        return lax.all_to_all(v, CHIPS, split_axis=0, concat_axis=0, tiled=True)

    spread = exchange(mine.reshape(16, SHARD // 16, D))
    summed = jnp.sum(spread.astype(F32), axis=0, keepdims=True).astype(BF)
    mine = exchange(jnp.broadcast_to(summed, (16, SHARD // 16, D))).reshape(SHARD, D)
    theirs = swap(mine)
    pair0 = jnp.where(first, mine, theirs).astype(F32) * (1.0 / 128.0)
    pair1 = jnp.where(first, theirs, mine).astype(F32) * (1.0 / 128.0)
    grad_w_in = jnp.stack(
        [pair0[:128].reshape(128, 4, DH), pair1[:128].reshape(128, 4, DH)], axis=2
    ).reshape(128, 2 * D)

    def unfold(v):
        return jnp.concatenate([v[128:160, :512], v[128:160, 512:]], axis=0)

    grad_w_out = jnp.concatenate([unfold(pair0), unfold(pair1)], axis=1)
    grad_bias = jnp.stack([v[160, :128] + v[160, 128:256] for v in (pair0, pair1)])
    return input_gradient, grad_w_in, grad_w_out, grad_bias


def solution(mesh):
    fine = Mesh(mesh.devices.reshape(2, 2, 2, 4, 8), ("yh", "core", "yl", "x", "z"))
    events = P(("yh", "core", "z"), ("yl", "x"), None)
    slots = P(("yh", "core", "z"))
    return jax.shard_map(
        local,
        mesh=fine,
        in_specs=(
            events,
            slots,
            slots,
            P(("yh", "core", "z"), ("yl", "x")),
            P("z", None),
            P("z", None),
            P(),
            events,
        ),
        out_specs=(events, P("z", None), P("z", None), P()),
        check_vma=False,
    )
```

```python
import functools

import jax
import jax.numpy as jnp
from jax import lax
from jax.experimental import pallas as pl
from jax.experimental.pallas import tpu as pltpu
from jax.sharding import Mesh
from jax.sharding import PartitionSpec as P

DH = 256
D = 1024
L = 1024
EPS = 1e-05
BF = jnp.bfloat16
F32 = jnp.float32
BQ = 256
NQ = L // BQ
SHARD = 1408
PLANE = ("yh", "core", "yl", "x")
CHIPS = ("yh", "yl", "x")
ANY = pl.BlockSpec(memory_space=pl.ANY)
VM = pl.BlockSpec(memory_space=pltpu.VMEM)
SM = pl.BlockSpec(memory_space=pltpu.SMEM)


def params(mib):
    return pltpu.CompilerParams(vmem_limit_bytes=mib << 20)


def shape(dims, kind):
    return jax.ShapeDtypeStruct(dims, kind)


def nn(a, b):
    return lax.dot_general(a, b, (((1,), (0,)), ((), ())), preferred_element_type=F32)


def nt(a, b):
    return lax.dot_general(a, b, (((1,), (1,)), ((), ())), preferred_element_type=F32)


def tn(a, b):
    return lax.dot_general(a, b, (((0,), (0,)), ((), ())), preferred_element_type=F32)


def rows(start, size):
    return pl.ds(pl.multiple_of(start, size), size)


def run_copies(copies):
    for c in copies:
        c.start()
    for c in copies:
        c.wait()


def unit_of(raw):
    yh, core, yl, x = raw[0], raw[1], raw[2], raw[3]
    e = 2 * yh + jnp.bitwise_and(x, 1)
    p = 2 * yl + jnp.bitwise_xor(lax.shift_right_logical(x, 1), yh)
    return e, p, core


def prepare_kernel(raw, plan, lay, w_in, w_out, *refs):
    outs, wsel, sem = refs[:4], refs[4], refs[5]
    copies = [
        pltpu.make_async_copy(
            lay.at[plan[jnp.bitwise_xor(raw[3], k)]], outs[k], sem.at[k]
        )
        for k in range(4)
    ]
    for c in copies:
        c.start()
    for head in range(2):

        @pl.when(raw[1] == head)
        def _(head=head):
            for c in range(4):
                wsel[0:128, 256 * c : 256 * c + 256] = w_in[
                    :, 512 * c + 256 * head : 512 * c + 256 * head + 256
                ]
            cols = slice(512 * head, 512 * head + 512)
            wsel[128:160, 0:512] = w_out[0:32, cols]
            wsel[128:160, 512:1024] = w_out[32:64, cols]

    for c in copies:
        c.wait()


def prepare(raw, plan, lay, w_in, w_out):
    return pl.pallas_call(
        prepare_kernel,
        out_shape=[shape((128, D), BF)] * 4 + [shape((160, D), BF)],
        in_specs=[SM, SM, ANY, VM, VM],
        out_specs=[VM] * 5,
        scratch_shapes=[pltpu.SemaphoreType.DMA((4,))],
        compiler_params=params(48),
        name="prepare",
    )(raw, plan, lay, w_in, w_out)


def pick_kernel(raw, lengths, grad, stamps, *refs):
    outs, sem = refs[:4], refs[4]
    slots = [jnp.bitwise_xor(raw[3], k) for k in range(4)]
    copies = [
        pltpu.make_async_copy(grad.at[slots[k]], outs[k].at[pl.ds(0, 128)], sem.at[k])
        for k in range(4)
    ]
    for c in copies:
        c.start()
    here = (raw[2] * 4 + raw[3]) * 128 + lax.broadcasted_iota(jnp.int32, (16, 128), 1)
    line = lax.broadcasted_iota(jnp.int32, (16, 128), 0)
    for k in range(4):
        time = jnp.broadcast_to(stamps[pl.ds(slots[k], 1), :].astype(F32), (16, 128))
        alive = jnp.where(here < lengths[slots[k]], 1.0, 0.0)
        value = jnp.where(line == 0, time, jnp.where(line == 1, alive, 0.0))
        outs[k][128:144, 0:128] = value.astype(BF)
        outs[k][128:144, 128:1024] = jnp.zeros((16, 896), BF)
    for c in copies:
        c.wait()


def pick(raw, lengths, grad, stamps):
    return pl.pallas_call(
        pick_kernel,
        out_shape=[shape((144, D), BF)] * 4,
        in_specs=[SM, SM, ANY, VM],
        out_specs=[VM] * 4,
        scratch_shapes=[pltpu.SemaphoreType.DMA((4,))],
        compiler_params=params(48),
        name="pick",
    )(raw, lengths, grad, stamps)


def block_of(h, other, k):
    half = h if k < 4 else 1 - h
    return half * 4 + jnp.bitwise_xor(other, k % 4)


def load_grad(gs, grad, p, h, sem, first):
    return [
        pltpu.make_async_copy(
            gs[k].at[pl.ds(0, 128)],
            grad.at[rows(block_of(h, p, k) * 128, 128)],
            sem.at[first + k],
        )
        for k in range(8)
    ]


def load_weights(wag, w, sem, first):
    return [
        pltpu.make_async_copy(
            wag.at[pl.ds(160 * z, 128)], w.at[pl.ds(128 * z, 128)], sem.at[first + z]
        )
        for z in range(8)
    ]


def forward_kernel(raw, tb, *refs):
    xs, gs, wag = refs[:8], refs[8:16], refs[16]
    normed, act, slope, probs, pslope, mixed, stats = refs[17:24]
    x, w, nv, av, sv, pv, qv, small, scol, srow, sem, out_sem = refs[24:]
    e, p, h = unit_of(raw)
    copies = load_weights(wag, w, sem, 0)
    for k in range(8):
        copies.append(
            pltpu.make_async_copy(
                xs[k], x.at[rows(block_of(h, e, k) * 128, 128)], sem.at[8 + k]
            )
        )
        copies.append(
            pltpu.make_async_copy(
                gs[k].at[pl.ds(128, 16), pl.ds(0, 128)],
                small.at[block_of(h, p, k)],
                sem.at[16 + k],
            )
        )
    run_copies(copies)
    leaving = []

    def leave(source, target):
        c = pltpu.make_async_copy(source, target, out_sem.at[len(leaving)])
        c.start()
        leaving.append(c)

    for i in range(NQ):
        at = pl.ds(i * BQ, BQ)
        v = x[at, :].astype(F32)
        v = v - jnp.mean(v, axis=-1, keepdims=True)
        r = lax.rsqrt(jnp.mean(v * v, axis=-1, keepdims=True) + EPS)
        n = (v * r).astype(BF)
        nv[at, :] = n
        stats[at, :] = jnp.broadcast_to(r, (BQ, 128))
        for c in range(4):
            cols = pl.ds(256 * c, 256)
            hidden = nn(n, w[:, cols])
            sg = jax.nn.sigmoid(hidden)
            av[at, cols] = (hidden * sg).astype(BF)
            sv[at, cols] = (sg * (1.0 + hidden * (1.0 - sg))).astype(BF)
        for source, target in ((nv, normed), (av, act), (sv, slope)):
            leave(source.at[at], target.at[at])

    for b in range(8):
        tile = small[b].astype(F32)
        srow[0:8, pl.ds(128 * b, 128)] = tile[0:8]
        full = jnp.concatenate([tile, jnp.zeros((112, 128), F32)], axis=0)
        scol[pl.ds(128 * b, 128), :] = jnp.transpose(full)

    both = tb[...].astype(F32)
    table = jnp.broadcast_to(jnp.where(h == 0, both[0:1], both[1:2]), (BQ, 128))
    lane = lax.broadcasted_iota(jnp.int32, (BQ, 128), 1)
    causal = (
        lax.broadcasted_iota(jnp.int32, (BQ, BQ), 1)
        <= lax.broadcasted_iota(jnp.int32, (BQ, BQ), 0)
    )
    for i in range(NQ):
        at = pl.ds(i * BQ, BQ)
        q = (av[at, 512:768].astype(F32) * (DH**-0.5)).astype(BF)
        si = scol[at, 0:1]
        lv = scol[at, 1:2]
        for j in range(i + 1):
            cols = pl.ds(j * BQ, BQ)
            s = nt(q, av[cols, 768:1024])
            near = jnp.clip(si - srow[0:1, cols], 0.0, 127.0).astype(jnp.int32)
            bias = jnp.concatenate(
                [
                    jnp.take_along_axis(table, near[:, :128], axis=1, mode="promise_in_bounds"),
                    jnp.take_along_axis(table, near[:, 128:], axis=1, mode="promise_in_bounds"),
                ],
                axis=1,
            )
            s = s + bias
            sg = jax.nn.sigmoid(s)
            live = jnp.where(causal, lv, 0.0) if j == i else lv
            pv[at, cols] = (s * sg * live).astype(BF)
            qv[at, cols] = (sg * (1.0 + s * (1.0 - sg)) * live).astype(BF)
        upto = (i + 1) * BQ
        for source, target in ((pv, probs), (qv, pslope)):
            leave(source.at[at, pl.ds(0, upto)], target.at[at, pl.ds(0, upto)])
        mixed[at, :] = nn(pv[at, 0:upto], av[0:upto, 256:512])
        stats[at, :] = jnp.where(lane == 5, si, stats[at, :])
    for c in leaving:
        c.wait()


def forward(raw, tb, xs, gs, wag):
    return pl.pallas_call(
        forward_kernel,
        out_shape=[shape((L, D), BF)] * 3
        + [shape((L, L), BF)] * 2
        + [shape((L, DH), F32), shape((L, 128), F32)],
        in_specs=[SM, VM] + [ANY] * 17,
        out_specs=[ANY] * 5 + [VM] * 2,
        scratch_shapes=[
            pltpu.VMEM((L, D), BF),
            pltpu.VMEM((D, D), BF),
            pltpu.VMEM((L, D), BF),
            pltpu.VMEM((L, D), BF),
            pltpu.VMEM((L, D), BF),
            pltpu.VMEM((L, L), BF),
            pltpu.VMEM((L, L), BF),
            pltpu.VMEM((8, 16, 128), BF),
            pltpu.VMEM((L, 128), F32),
            pltpu.VMEM((8, L), F32),
            pltpu.SemaphoreType.DMA((24,)),
            pltpu.SemaphoreType.DMA((20,)),
        ],
        compiler_params=params(56),
        name="forward",
    )(raw, tb, *xs, *gs, wag)


def whole(*dims):
    return pl.BlockSpec(dims, lambda i: (0,) * len(dims))


FIRST = pl.BlockSpec((L, DH), lambda i: (0, 0))


def statistics_kernel(raw, mixed, gate, base, *refs):
    gs, wag, wrecv = refs[:8], refs[8], refs[9]
    dz, stats, grad, wo, sem = refs[10:]
    _, p, h = unit_of(raw)
    copies = load_grad(gs, grad, p, h, sem, 0)
    for q in range(4):
        for r in range(2):
            own = wag.at[
                pl.ds(pl.multiple_of((4 * h + q) * 160 + 128, 32), 32), pl.ds(512 * r, 512)
            ]
            other = wrecv.at[q, :, pl.ds(512 * r, 512)]
            to = pl.ds(64 * q + 32 * r, 32)
            copies.append(
                pltpu.make_async_copy(own, wo.at[to, rows(h * 512, 512)], sem.at[8 + 4 * q + r])
            )
            copies.append(
                pltpu.make_async_copy(
                    other, wo.at[to, rows((1 - h) * 512, 512)], sem.at[10 + 4 * q + r]
                )
            )
    run_copies(copies)
    lane = lax.broadcasted_iota(jnp.int32, (BQ, 128), 1)
    for i in range(NQ):
        at = pl.ds(i * BQ, BQ)
        d = nt(grad[at, :], wo[...])
        dz[at, :] = d
        gated = mixed[at, :] * gate[at, :].astype(F32)
        m = jnp.mean(gated, axis=-1, keepdims=True)
        centred = gated - m
        m2 = jnp.sum(centred * centred, axis=-1, keepdims=True)
        s3 = jnp.sum(d, axis=-1, keepdims=True)
        s4 = jnp.sum(d * centred, axis=-1, keepdims=True)
        row = base[at, :]
        for n, value in enumerate((m, m2, s3, s4)):
            row = jnp.where(lane == n, value, row)
        stats[at, :] = row


def statistics(raw, mixed, act, base, gs, wag, wrecv):
    return pl.pallas_call(
        statistics_kernel,
        grid=(1,),
        out_shape=[shape((L, DH), F32), shape((L, 128), F32)],
        in_specs=[SM, whole(L, DH), FIRST, whole(L, 128)] + [ANY] * 10,
        out_specs=[whole(L, DH), whole(L, 128)],
        scratch_shapes=[
            pltpu.VMEM((L, D), BF),
            pltpu.VMEM((DH, D), BF),
            pltpu.SemaphoreType.DMA((24,)),
        ],
        compiler_params=params(56),
        name="statistics",
    )(raw, mixed, act, base, *gs, wag, wrecv)


def middle_kernel(raw, own, peer, mixed, dz, gate, gslope, *refs):
    gs = refs[:8]
    datt, dhu, keep, send, zl, grad, sem = refs[8:]
    _, p, h = unit_of(raw)
    copies = load_grad(gs, grad, p, h, sem, 0)
    for c in copies:
        c.start()
    for i in range(NQ):
        at = pl.ds(i * BQ, BQ)
        a, b = own[at, :], peer[at, :]
        m0, m1 = a[:, 0:1], b[:, 0:1]
        mean = 0.5 * (m0 + m1)
        gap = m0 - mean
        r = lax.rsqrt((a[:, 1:2] + b[:, 1:2] + 512.0 * gap * gap) * (1.0 / 512.0) + EPS)
        dmean = (a[:, 2:3] + b[:, 2:3]) * (1.0 / 512.0)
        cross = a[:, 3:4] + b[:, 3:4] + gap * (a[:, 2:3] - b[:, 2:3])
        cross = cross * r * (1.0 / 512.0)
        mix = mixed[at, :]
        u = gate[at, :].astype(F32)
        zhat = (mix * u - mean) * r
        zl[at, :] = zhat.astype(BF)
        dgated = r * (dz[at, :] - dmean - zhat * cross)
        datt[at, :] = (dgated * u).astype(BF)
        dhu[at, :] = (dgated * mix * gslope[at, :].astype(F32)).astype(BF)
    for c in copies:
        c.wait()
    for half in range(2):
        po = tn(zl[...], grad[:, 512 * half : 512 * half + 512]).astype(BF)
        for q in range(4):
            block = jnp.concatenate(
                [po[64 * q : 64 * q + 32], po[64 * q + 32 : 64 * q + 64]], axis=1
            )

            @pl.when(h == half)
            def _(block=block, q=q):
                keep[q] = block

            @pl.when(h != half)
            def _(block=block, q=q):
                send[q] = block


def middle(raw, own, peer, mixed, dz, act, slope, gs):
    return pl.pallas_call(
        middle_kernel,
        grid=(1,),
        out_shape=[shape((L, DH), BF)] * 2 + [shape((4, 32, D), BF)] * 2,
        in_specs=[SM, whole(L, 128), whole(L, 128), whole(L, DH), whole(L, DH), FIRST, FIRST]
        + [ANY] * 8,
        out_specs=[whole(L, DH), whole(L, DH), whole(4, 32, D), whole(4, 32, D)],
        scratch_shapes=[
            pltpu.VMEM((L, DH), BF),
            pltpu.VMEM((L, D), BF),
            pltpu.SemaphoreType.DMA((8,)),
        ],
        compiler_params=params(56),
        name="middle",
    )(raw, own, peer, mixed, dz, act, slope, *gs)


def backward_kernel(
    raw, act_in, slope_in, probs_in, pslope_in, normed_in, datt, dhu, stats, keep, recv, *refs
):
    part, dhid_out, act, slope, probs, pslope, normed, dhid, dlow, hot, sem = refs
    h = raw[1]
    sources = (act_in, pslope_in, slope_in, probs_in, normed_in)
    targets = (act, pslope, slope, probs, normed)
    copies = [
        pltpu.make_async_copy(a, b, sem.at[n]) for n, (a, b) in enumerate(zip(sources, targets))
    ]
    for c in copies:
        c.start()
    stamp_lane = lax.broadcasted_iota(jnp.int32, (L, 256), 1).astype(F32)
    hot[...] = jnp.where(stats[:, 5:6] == stamp_lane, 1.0, 0.0).astype(BF)
    dhid[:, 0:256] = dhu[...]
    bucket = lax.broadcasted_iota(jnp.int32, (BQ, 128), 1)
    time = lax.broadcasted_iota(jnp.int32, (BQ, 256), 1)
    total = jnp.zeros((BQ, 128), F32)
    for c in copies[:3]:
        c.wait()
    for i in range(NQ):
        at = pl.ds(i * BQ, BQ)
        upto = (i + 1) * BQ
        da = datt[at, :]
        for j in range(i + 1):
            cols = pl.ds(j * BQ, BQ)
            dp = nt(da, act[cols, 256:512])
            dlow[at, cols] = (dp * pslope[at, cols].astype(F32)).astype(BF)
        low = dlow[at, 0:upto]
        dq = nn(low, act[0:upto, 768:1024]) * (DH**-0.5)
        dhid[at, 512:768] = (dq * slope[at, 512:768].astype(F32)).astype(BF)
        by_time = nn(low, hot[0:upto, :])
        si = stats[at, 5:6].astype(jnp.int32)
        when = si - bucket
        index = jnp.bitwise_and(when, 127)
        early = jnp.take_along_axis(by_time[:, :128], index, axis=1, mode="promise_in_bounds")
        late = jnp.take_along_axis(by_time[:, 128:], index, axis=1, mode="promise_in_bounds")
        picked = jnp.where(when >= 128, late, jnp.where(when >= 0, early, 0.0))
        far = jnp.sum(jnp.where(time <= si - 127, by_time, 0.0), axis=-1, keepdims=True)
        total = total + jnp.where(bucket == 127, far, picked)
    copies[3].wait()
    for j in range(NQ):
        cols = pl.ds(j * BQ, BQ)
        frm = j * BQ
        dv = tn(probs[frm:, cols], datt[frm:, :])
        dhid[cols, 256:512] = (dv * slope[cols, 256:512].astype(F32)).astype(BF)
        dk = tn(dlow[frm:, cols], act[frm:, 512:768]) * (DH**-0.5)
        dhid[cols, 768:1024] = (dk * slope[cols, 768:1024].astype(F32)).astype(BF)
    leaving = pltpu.make_async_copy(dhid, dhid_out, sem.at[5])
    leaving.start()
    copies[4].wait()
    for b in range(4):
        for c in range(4):
            pin = tn(normed[:, 256 * b : 256 * b + 256], dhid[:, pl.ds(256 * c, 256)]).astype(BF)
            for z in range(2):
                for t in range(2):
                    start = (2 * b + z) * SHARD + 128 * (2 * c + t)
                    part[pl.ds(start, 128), :] = pin[
                        128 * z : 128 * z + 128, 128 * t : 128 * t + 128
                    ]
    bias = jnp.sum(total, axis=0, keepdims=True)
    high = bias.astype(BF).astype(F32)
    line = lax.broadcasted_iota(jnp.int32, (128, 128), 0)
    tile = jnp.where(line == 0, high, jnp.where(line == 1, bias - high, 0.0)).astype(BF)
    for z in range(8):
        part[pl.ds(z * SHARD + 1280, 128), :] = tile
    for q in range(4):
        for t in range(8):
            mine = pl.multiple_of((4 * h + q) * SHARD + 1024 + 32 * t, 32)
            theirs = pl.multiple_of((4 * (1 - h) + q) * SHARD + 1024 + 32 * t, 32)
            part[pl.ds(mine, 32), :] = keep[q, :, 128 * t : 128 * t + 128]
            part[pl.ds(theirs, 32), :] = recv[q, :, 128 * t : 128 * t + 128]
    leaving.wait()


def backward(raw, act, slope, probs, pslope, normed, datt, dhu, stats, keep, recv):
    return pl.pallas_call(
        backward_kernel,
        out_shape=[shape((8 * SHARD, 128), BF), shape((L, D), BF)],
        in_specs=[SM] + [ANY] * 5 + [VM] * 5,
        out_specs=[VM, ANY],
        scratch_shapes=[
            pltpu.VMEM((L, D), BF),
            pltpu.VMEM((L, D), BF),
            pltpu.VMEM((L, L), BF),
            pltpu.VMEM((L, L), BF),
            pltpu.VMEM((L, D), BF),
            pltpu.VMEM((L, D), BF),
            pltpu.VMEM((L, L), BF),
            pltpu.VMEM((L, 256), BF),
            pltpu.SemaphoreType.DMA((6,)),
        ],
        compiler_params=params(56),
        name="backward",
    )(raw, act, slope, probs, pslope, normed, datt, dhu, stats, keep, recv)


def input_kernel(raw, dhid, normed, stats, wag, own, other, w, sem):
    h = raw[1]
    run_copies(load_weights(wag, w, sem, 0))
    for i in range(NQ):
        at = pl.ds(i * BQ, BQ)
        dn = nt(dhid[at, :], w[...])
        n = normed[at, :].astype(F32)
        r = stats[at, 4:5]
        mean = jnp.mean(dn, axis=-1, keepdims=True)
        cross = jnp.mean(dn * n, axis=-1, keepdims=True)
        res = (r * (dn - mean - n * cross)).astype(BF)
        to = pl.ds((i % 2) * BQ, BQ)

        @pl.when(h == i // 2)
        def _(res=res, to=to):
            own[to, :] = res

        @pl.when(h != i // 2)
        def _(res=res, to=to):
            other[to, :] = res


def input_grad(raw, dhid, normed, stats, wag):
    return pl.pallas_call(
        input_kernel,
        out_shape=[shape((512, D), BF)] * 2,
        in_specs=[SM] + [VM] * 3 + [ANY],
        out_specs=[VM, VM],
        scratch_shapes=[pltpu.VMEM((D, D), BF), pltpu.SemaphoreType.DMA((8,))],
        compiler_params=params(48),
        name="input_grad",
    )(raw, dhid, normed, stats, wag)


def add_kernel(raw, a, b, *outs):
    _, p, _ = unit_of(raw)
    for k in range(4):
        at = rows(jnp.bitwise_xor(p, k) * 128, 128)
        outs[k][...] = (a[at, :].astype(F32) + b[at, :].astype(F32)).astype(BF)


def add_halves(raw, a, b):
    return pl.pallas_call(
        add_kernel,
        out_shape=[shape((128, D), BF)] * 4,
        in_specs=[SM, VM, VM],
        out_specs=[VM] * 4,
        compiler_params=params(48),
        name="add_halves",
    )(raw, a, b)


def place_kernel(raw, *refs):
    chunks, out, sem = refs[:4], refs[4], refs[5]
    run_copies(
        [
            pltpu.make_async_copy(chunks[k], out.at[jnp.bitwise_xor(raw[3], k)], sem.at[k])
            for k in range(4)
        ]
    )


def place(raw, chunks):
    return pl.pallas_call(
        place_kernel,
        out_shape=shape((4, 128, D), BF),
        in_specs=[SM] + [ANY] * 4,
        out_specs=VM,
        scratch_shapes=[pltpu.SemaphoreType.DMA((4,))],
        compiler_params=params(48),
        name="place",
    )(raw, *chunks)


def finish_kernel(raw, mine, theirs, w_in, w_out, bias):
    for core in range(2):

        @pl.when(raw[1] == core)
        def _(core=core):
            for side, src in ((core, mine), (1 - core, theirs)):
                for t in range(8):
                    col = 512 * (t // 2) + 256 * side + 128 * (t % 2)
                    w_in[:, col : col + 128] = src[128 * t : 128 * t + 128, :].astype(F32) / 128.0
                    at = 1024 + 32 * t
                    row, col = 32 * (t // 4), 512 * side + 128 * (t % 4)
                    w_out[row : row + 32, col : col + 128] = (
                        src[at : at + 32, :].astype(F32) / 128.0
                    )
                tail = src[1280:1296, :].astype(F32)
                bias[side : side + 1, :] = (tail[0:1] + tail[1:2]) / 128.0


def finish(raw, mine, theirs):
    return pl.pallas_call(
        finish_kernel,
        out_shape=[shape((128, 2 * D), F32), shape((64, D), F32), shape((2, 128), F32)],
        in_specs=[SM, VM, VM],
        out_specs=[VM] * 3,
        compiler_params=params(48),
        name="finish",
    )(raw, mine, theirs)


def device(yh, core, yl, x):
    return ((yh * 2 + core) * 2 + yl) * 4 + x


def unit_device(e, p, half):
    ye, ce = e >> 1, e & 1
    yp, cp = p >> 1, p & 1
    return device(ye, half, yp, 2 * (ye ^ cp) + ce)


def input_pairs(k):
    pairs = []
    for p in range(4):
        for yl in range(2):
            for x in range(4):
                pairs.append((device(p >> 1, p & 1, yl, x), unit_device(x ^ k, p, yl)))
    return pairs


def grad_pairs(k):
    pairs = []
    for e in range(4):
        for yl in range(2):
            for x in range(4):
                pairs.append((device(e >> 1, e & 1, yl, x), unit_device(e, x ^ k, yl)))
    return pairs


def back_pairs(k):
    return [(b, a) for a, b in grad_pairs(k)]


def local(layer_in, repack_plan, lengths, stamps, w_in, w_out, time_bias, grad_out):
    raw = jnp.stack([lax.axis_index(n).astype(jnp.int32) for n in PLANE])
    first = lax.axis_index("core") == 0
    swap = functools.partial(lax.ppermute, axis_name="core", perm=[(0, 1), (1, 0)])

    *chunks, wsel = prepare(raw, repack_plan, layer_in, w_in, w_out)
    wag = lax.all_gather(wsel, "z", axis=0, tiled=True)
    xs = [lax.ppermute(c, PLANE, input_pairs(k)) for k, c in enumerate(chunks)]
    picked = pick(raw, lengths, grad_out, stamps)
    gs = [lax.ppermute(c, PLANE, grad_pairs(k)) for k, c in enumerate(picked)]
    xs = xs + [swap(c) for c in xs]
    gs = gs + [swap(c) for c in gs]
    w3 = wag.reshape(8, 160, D)
    wrecv = swap(jnp.where(first, w3[4:, 128:], w3[:4, 128:]))

    normed, act, slope, probs, pslope, mixed, base = forward(raw, time_bias, xs, gs, wag)
    dz, stats = statistics(raw, mixed, act, base, gs, wag, wrecv)
    datt, dhu, keep, send = middle(raw, stats, swap(stats), mixed, dz, act, slope, gs)
    part, dhid = backward(
        raw, act, slope, probs, pslope, normed, datt, dhu, stats, keep, swap(send)
    )
    mine = lax.psum_scatter(part, "z", scatter_dimension=0, tiled=True)
    own, other = input_grad(raw, dhid, normed, stats, wag)
    pieces = add_halves(raw, own, swap(other))
    back = [lax.ppermute(pieces[k], PLANE, back_pairs(k)) for k in range(4)]
    input_gradient = place(raw, back)
    mine, input_gradient = lax.optimization_barrier((mine, input_gradient))

    def exchange(v):
        return lax.all_to_all(v, CHIPS, split_axis=0, concat_axis=0, tiled=True)

    spread = exchange(mine.reshape(16, SHARD // 16, 128))
    summed = jnp.sum(spread.astype(F32), axis=0, keepdims=True).astype(BF)
    mine = exchange(jnp.broadcast_to(summed, spread.shape)).reshape(SHARD, 128)
    grad_w_in, grad_w_out, grad_bias = finish(raw, mine, swap(mine))
    return input_gradient, grad_w_in, grad_w_out, grad_bias


def solution(mesh):
    fine = Mesh(mesh.devices.reshape(2, 2, 2, 4, 8), ("yh", "core", "yl", "x", "z"))
    events = P(("yh", "core", "z"), ("yl", "x"), None)
    slots = P(("yh", "core", "z"))
    return jax.shard_map(
        local,
        mesh=fine,
        in_specs=(
            events,
            slots,
            slots,
            P(("yh", "core", "z"), ("yl", "x")),
            P("z", None),
            P("z", None),
            P(),
            events,
        ),
        out_specs=(events, P("z", None), P("z", None), P()),
        check_vma=False,
    )
```

```python
import functools

import jax
import jax.numpy as jnp
from jax import lax
from jax.experimental import pallas as pl
from jax.experimental.pallas import tpu as pltpu
from jax.sharding import Mesh
from jax.sharding import PartitionSpec as P

DH = 256
D = 1024
L = 1024
EPS = 1e-05
BF = jnp.bfloat16
F32 = jnp.float32
BQ = 256
NQ = L // BQ
SHARD = 1408
PLANE = ("yh", "core", "yl", "x")
CHIPS = ("yh", "yl", "x")
ANY = pl.BlockSpec(memory_space=pl.ANY)
VM = pl.BlockSpec(memory_space=pltpu.VMEM)
SM = pl.BlockSpec(memory_space=pltpu.SMEM)


def params(mib):
    return pltpu.CompilerParams(vmem_limit_bytes=mib << 20)


def shape(dims, kind):
    return jax.ShapeDtypeStruct(dims, kind)


def nn(a, b):
    return lax.dot_general(a, b, (((1,), (0,)), ((), ())), preferred_element_type=F32)


def nt(a, b):
    return lax.dot_general(a, b, (((1,), (1,)), ((), ())), preferred_element_type=F32)


def tn(a, b):
    return lax.dot_general(a, b, (((0,), (0,)), ((), ())), preferred_element_type=F32)


def rows(start, size):
    return pl.ds(pl.multiple_of(start, size), size)


def run_copies(copies):
    for c in copies:
        c.start()
    for c in copies:
        c.wait()


def unit_of():
    yh, core, yl, x = (lax.axis_index(n) for n in PLANE)
    e = 2 * yh + jnp.bitwise_and(x, 1)
    p = 2 * yl + jnp.bitwise_xor(lax.shift_right_logical(x, 1), yh)
    return e, p, core


def prepare_kernel(plan, lay, w_in, w_out, *refs):
    outs, wsel, sem = refs[:4], refs[4], refs[5]
    h = lax.axis_index("core")
    weights = [
        pltpu.make_async_copy(
            w_in.at[:, rows(512 * c + 256 * h, 256)],
            wsel.at[pl.ds(0, 128), pl.ds(256 * c, 256)],
            sem.at[4 + c],
        )
        for c in range(4)
    ] + [
        pltpu.make_async_copy(
            w_out.at[pl.ds(32 * r, 32), rows(512 * h, 512)],
            wsel.at[pl.ds(128, 32), pl.ds(512 * r, 512)],
            sem.at[8 + r],
        )
        for r in range(2)
    ]
    copies = weights + [
        pltpu.make_async_copy(
            lay.at[plan[jnp.bitwise_xor(lax.axis_index("x"), k)]], outs[k], sem.at[k]
        )
        for k in range(4)
    ]
    run_copies(copies)


def prepare(plan, lay, w_in, w_out):
    return pl.pallas_call(
        prepare_kernel,
        out_shape=[shape((128, D), BF)] * 4 + [shape((160, D), BF)],
        in_specs=[SM, ANY, ANY, ANY],
        out_specs=[VM] * 5,
        scratch_shapes=[pltpu.SemaphoreType.DMA((10,))],
        compiler_params=params(60),
        name="prepare",
    )(plan, lay, w_in, w_out)


def pick_kernel(lengths, grad, stamps, *refs):
    outs, sem = refs[:4], refs[4]
    slots = [jnp.bitwise_xor(lax.axis_index("x"), k) for k in range(4)]
    copies = [
        pltpu.make_async_copy(grad.at[slots[k]], outs[k].at[pl.ds(0, 128)], sem.at[k])
        for k in range(4)
    ]
    for c in copies:
        c.start()
    here = (lax.axis_index("yl") * 4 + lax.axis_index("x")) * 128 + lax.broadcasted_iota(jnp.int32, (16, 128), 1)
    line = lax.broadcasted_iota(jnp.int32, (16, 128), 0)
    for k in range(4):
        time = jnp.broadcast_to(stamps[pl.ds(slots[k], 1), :].astype(F32), (16, 128))
        alive = jnp.where(here < lengths[slots[k]], 1.0, 0.0)
        value = jnp.where(line == 0, time, jnp.where(line == 1, alive, 0.0))
        outs[k][128:144, 0:128] = value.astype(BF)
        outs[k][128:144, 128:1024] = jnp.zeros((16, 896), BF)
    for c in copies:
        c.wait()


def pick(lengths, grad, stamps):
    return pl.pallas_call(
        pick_kernel,
        out_shape=[shape((144, D), BF)] * 4,
        in_specs=[SM, ANY, VM],
        out_specs=[VM] * 4,
        scratch_shapes=[pltpu.SemaphoreType.DMA((4,))],
        compiler_params=params(60),
        name="pick",
    )(lengths, grad, stamps)


def block_of(h, other, k):
    half = h if k < 4 else 1 - h
    return half * 4 + jnp.bitwise_xor(other, k % 4)


def load_grad(gs, grad, p, h, sem, first):
    return [
        pltpu.make_async_copy(
            gs[k].at[pl.ds(0, 128)],
            grad.at[rows(block_of(h, p, k) * 128, 128)],
            sem.at[first + k],
        )
        for k in range(8)
    ]


def load_weights(wag, w, sem, first):
    return [
        pltpu.make_async_copy(
            wag.at[pl.ds(160 * z, 128)], w.at[pl.ds(128 * z, 128)], sem.at[first + z]
        )
        for z in range(8)
    ]


def forward_kernel(tb, *refs):
    xs, gs, wag, wrecv = refs[:8], refs[8:16], refs[16], refs[17]
    normed, act, slope, probs, pslope, mixed, dz, stats = refs[18:26]
    x, w, nv, av, sv, pv, qv, grad, wo, small, scol, srow, sem, out_sem = refs[26:]
    e, p, h = unit_of()
    copies = load_weights(wag, w, sem, 0)
    for k in range(8):
        copies.append(
            pltpu.make_async_copy(
                xs[k], x.at[rows(block_of(h, e, k) * 128, 128)], sem.at[8 + k]
            )
        )
        copies.append(
            pltpu.make_async_copy(
                gs[k].at[pl.ds(128, 16), pl.ds(0, 128)],
                small.at[block_of(h, p, k)],
                sem.at[16 + k],
            )
        )
    late = load_grad(gs, grad, p, h, sem, 24)
    for q in range(4):
        for r in range(2):
            own = wag.at[
                pl.ds(pl.multiple_of((4 * h + q) * 160 + 128, 32), 32), pl.ds(512 * r, 512)
            ]
            other = wrecv.at[q, :, pl.ds(512 * r, 512)]
            to = pl.ds(64 * q + 32 * r, 32)
            n = 32 + 4 * q + 2 * r
            late.append(
                pltpu.make_async_copy(own, wo.at[to, rows(h * 512, 512)], sem.at[n])
            )
            late.append(
                pltpu.make_async_copy(other, wo.at[to, rows((1 - h) * 512, 512)], sem.at[n + 1])
            )
    for c in copies + late:
        c.start()
    for c in copies:
        c.wait()
    leaving = []

    def leave(source, target):
        c = pltpu.make_async_copy(source, target, out_sem.at[len(leaving)])
        c.start()
        leaving.append(c)

    for i in range(NQ):
        at = pl.ds(i * BQ, BQ)
        v = x[at, :].astype(F32)
        v = v - jnp.mean(v, axis=-1, keepdims=True)
        r = lax.rsqrt(jnp.mean(v * v, axis=-1, keepdims=True) + EPS)
        n = (v * r).astype(BF)
        nv[at, :] = n
        stats[at, :] = jnp.broadcast_to(r, (BQ, 128))
        for c in range(4):
            cols = pl.ds(256 * c, 256)
            hidden = nn(n, w[:, cols])
            sg = jax.nn.sigmoid(hidden)
            av[at, cols] = (hidden * sg).astype(BF)
            sv[at, cols] = (sg * (1.0 + hidden * (1.0 - sg))).astype(BF)
        for source, target in ((nv, normed), (av, act), (sv, slope)):
            leave(source.at[at], target.at[at])

    for b in range(8):
        tile = small[b].astype(F32)
        srow[0:8, pl.ds(128 * b, 128)] = tile[0:8]
        full = jnp.concatenate([tile, jnp.zeros((112, 128), F32)], axis=0)
        scol[pl.ds(128 * b, 128), :] = jnp.transpose(full)

    both = tb[...].astype(F32)
    table = jnp.broadcast_to(jnp.where(h == 0, both[0:1], both[1:2]), (BQ, 128))
    lane = lax.broadcasted_iota(jnp.int32, (BQ, 128), 1)
    causal = (
        lax.broadcasted_iota(jnp.int32, (BQ, BQ), 1)
        <= lax.broadcasted_iota(jnp.int32, (BQ, BQ), 0)
    )
    for i in range(NQ):
        at = pl.ds(i * BQ, BQ)
        q = (av[at, 512:768].astype(F32) * (DH**-0.5)).astype(BF)
        si = scol[at, 0:1]
        lv = scol[at, 1:2]
        for j in range(i + 1):
            cols = pl.ds(j * BQ, BQ)
            s = nt(q, av[cols, 768:1024])
            near = jnp.clip(si - srow[0:1, cols], 0.0, 127.0).astype(jnp.int32)
            bias = jnp.concatenate(
                [
                    jnp.take_along_axis(table, near[:, :128], axis=1, mode="promise_in_bounds"),
                    jnp.take_along_axis(table, near[:, 128:], axis=1, mode="promise_in_bounds"),
                ],
                axis=1,
            )
            s = s + bias
            sg = jax.nn.sigmoid(s)
            live = jnp.where(causal, lv, 0.0) if j == i else lv
            pv[at, cols] = (s * sg * live).astype(BF)
            qv[at, cols] = (sg * (1.0 + s * (1.0 - sg)) * live).astype(BF)
        upto = (i + 1) * BQ
        for source, target in ((pv, probs), (qv, pslope)):
            leave(source.at[at, pl.ds(0, upto)], target.at[at, pl.ds(0, upto)])
        mixed[at, :] = nn(pv[at, 0:upto], av[0:upto, 256:512])
        stats[at, :] = jnp.where(lane == 5, si, stats[at, :])
    for c in late:
        c.wait()
    for i in range(NQ):
        at = pl.ds(i * BQ, BQ)
        d = nt(grad[at, :], wo[...])
        dz[at, :] = d
        gated = mixed[at, :] * av[at, 0:256].astype(F32)
        m = jnp.mean(gated, axis=-1, keepdims=True)
        centred = gated - m
        m2 = jnp.sum(centred * centred, axis=-1, keepdims=True)
        s3 = jnp.sum(d, axis=-1, keepdims=True)
        s4 = jnp.sum(d * centred, axis=-1, keepdims=True)
        row = stats[at, :]
        for n, value in enumerate((m, m2, s3, s4)):
            row = jnp.where(lane == n, value, row)
        stats[at, :] = row
    for c in leaving:
        c.wait()


def forward(tb, xs, gs, wag, wrecv):
    return pl.pallas_call(
        forward_kernel,
        out_shape=[shape((L, D), BF)] * 3
        + [shape((L, L), BF)] * 2
        + [shape((L, DH), F32)] * 2
        + [shape((L, 128), F32)],
        in_specs=[VM] + [ANY] * 18,
        out_specs=[ANY] * 5 + [VM] * 3,
        scratch_shapes=[
            pltpu.VMEM((L, D), BF),
            pltpu.VMEM((D, D), BF),
            pltpu.VMEM((L, D), BF),
            pltpu.VMEM((L, D), BF),
            pltpu.VMEM((L, D), BF),
            pltpu.VMEM((L, L), BF),
            pltpu.VMEM((L, L), BF),
            pltpu.VMEM((L, D), BF),
            pltpu.VMEM((DH, D), BF),
            pltpu.VMEM((8, 16, 128), BF),
            pltpu.VMEM((L, 128), F32),
            pltpu.VMEM((8, L), F32),
            pltpu.SemaphoreType.DMA((48,)),
            pltpu.SemaphoreType.DMA((20,)),
        ],
        compiler_params=params(34),
        name="forward",
    )(tb, *xs, *gs, wag, wrecv)


def whole(*dims):
    return pl.BlockSpec(dims, lambda i: (0,) * len(dims))


FIRST = pl.BlockSpec((L, DH), lambda i: (0, 0))


def middle_kernel(own, peer, mixed, dz, gate, gslope, *refs):
    gs = refs[:8]
    datt, dhu, keep, send, zl, grad, sem = refs[8:]
    _, p, h = unit_of()
    copies = load_grad(gs, grad, p, h, sem, 0)
    for c in copies:
        c.start()
    for i in range(NQ):
        at = pl.ds(i * BQ, BQ)
        a, b = own[at, :], peer[at, :]
        m0, m1 = a[:, 0:1], b[:, 0:1]
        mean = 0.5 * (m0 + m1)
        gap = m0 - mean
        r = lax.rsqrt((a[:, 1:2] + b[:, 1:2] + 512.0 * gap * gap) * (1.0 / 512.0) + EPS)
        dmean = (a[:, 2:3] + b[:, 2:3]) * (1.0 / 512.0)
        cross = a[:, 3:4] + b[:, 3:4] + gap * (a[:, 2:3] - b[:, 2:3])
        cross = cross * r * (1.0 / 512.0)
        mix = mixed[at, :]
        u = gate[at, :].astype(F32)
        zhat = (mix * u - mean) * r
        zl[at, :] = zhat.astype(BF)
        dgated = r * (dz[at, :] - dmean - zhat * cross)
        datt[at, :] = (dgated * u).astype(BF)
        dhu[at, :] = (dgated * mix * gslope[at, :].astype(F32)).astype(BF)
    for c in copies:
        c.wait()
    out = tn(zl[...], grad[...]).astype(BF)
    for half in range(2):
        for q in range(4):
            block = jnp.concatenate(
                [
                    out[64 * q + r : 64 * q + r + 32, 512 * half : 512 * half + 512]
                    for r in (0, 32)
                ],
                axis=1,
            )

            @pl.when(h == half)
            def _(block=block, q=q):
                keep[q] = block

            @pl.when(h != half)
            def _(block=block, q=q):
                send[q] = block


def middle(own, peer, mixed, dz, act, slope, gs):
    return pl.pallas_call(
        middle_kernel,
        grid=(1,),
        out_shape=[shape((L, DH), BF)] * 2 + [shape((4, 32, D), BF)] * 2,
        in_specs=[whole(L, 128), whole(L, 128), whole(L, DH), whole(L, DH), FIRST, FIRST]
        + [ANY] * 8,
        out_specs=[whole(L, DH), whole(L, DH), whole(4, 32, D), whole(4, 32, D)],
        scratch_shapes=[
            pltpu.VMEM((L, DH), BF),
            pltpu.VMEM((L, D), BF),
            pltpu.SemaphoreType.DMA((8,)),
        ],
        compiler_params=params(20),
        name="middle",
    )(own, peer, mixed, dz, act, slope, *gs)


def backward_kernel(
    act_in, slope_in, probs_in, pslope_in, normed_in, datt, dhu, stats, keep, recv, *refs
):
    part, dhid_out, act, slope, probs, pslope, normed, dhid, dlow, hot, sem = refs
    h = lax.axis_index("core")
    sources = (act_in, pslope_in, slope_in, probs_in, normed_in)
    targets = (act, pslope, slope, probs, normed)
    copies = [
        pltpu.make_async_copy(a, b, sem.at[n]) for n, (a, b) in enumerate(zip(sources, targets))
    ]
    for c in copies:
        c.start()
    stamp_lane = lax.broadcasted_iota(jnp.int32, (L, 256), 1).astype(F32)
    hot[...] = jnp.where(stats[:, 5:6] == stamp_lane, 1.0, 0.0).astype(BF)
    dhid[:, 0:256] = dhu[...]
    bucket = lax.broadcasted_iota(jnp.int32, (BQ, 128), 1)
    time = lax.broadcasted_iota(jnp.int32, (BQ, 256), 1)
    total = jnp.zeros((BQ, 128), F32)
    for c in copies[:3]:
        c.wait()
    for i in range(NQ):
        at = pl.ds(i * BQ, BQ)
        upto = (i + 1) * BQ
        da = datt[at, :]
        for j in range(i + 1):
            cols = pl.ds(j * BQ, BQ)
            dp = nt(da, act[cols, 256:512])
            dlow[at, cols] = (dp * pslope[at, cols].astype(F32)).astype(BF)
        low = dlow[at, 0:upto]
        dq = nn(low, act[0:upto, 768:1024]) * (DH**-0.5)
        dhid[at, 512:768] = (dq * slope[at, 512:768].astype(F32)).astype(BF)
        by_time = nn(low, hot[0:upto, :])
        si = stats[at, 5:6].astype(jnp.int32)
        when = si - bucket
        index = jnp.bitwise_and(when, 127)
        early = jnp.take_along_axis(by_time[:, :128], index, axis=1, mode="promise_in_bounds")
        late = jnp.take_along_axis(by_time[:, 128:], index, axis=1, mode="promise_in_bounds")
        picked = jnp.where(when >= 128, late, jnp.where(when >= 0, early, 0.0))
        far = jnp.sum(jnp.where(time <= si - 127, by_time, 0.0), axis=-1, keepdims=True)
        total = total + jnp.where(bucket == 127, far, picked)
    copies[3].wait()
    for j in range(NQ):
        cols = pl.ds(j * BQ, BQ)
        frm = j * BQ
        dv = tn(probs[frm:, cols], datt[frm:, :])
        dhid[cols, 256:512] = (dv * slope[cols, 256:512].astype(F32)).astype(BF)
        dk = tn(dlow[frm:, cols], act[frm:, 512:768]) * (DH**-0.5)
        dhid[cols, 768:1024] = (dk * slope[cols, 768:1024].astype(F32)).astype(BF)
    leaving = pltpu.make_async_copy(dhid, dhid_out, sem.at[5])
    leaving.start()
    copies[4].wait()
    for b in range(4):
        pin = tn(normed[:, 256 * b : 256 * b + 256], dhid[...]).astype(BF)
        for z in range(2):
            for t in range(8):
                part[pl.ds((2 * b + z) * SHARD + 128 * t, 128), :] = pin[
                    128 * z : 128 * z + 128, 128 * t : 128 * t + 128
                ]
    bias = jnp.sum(total, axis=0, keepdims=True)
    high = bias.astype(BF).astype(F32)
    line = lax.broadcasted_iota(jnp.int32, (128, 128), 0)
    tile = jnp.where(line == 0, high, jnp.where(line == 1, bias - high, 0.0)).astype(BF)
    for z in range(8):
        part[pl.ds(z * SHARD + 1280, 128), :] = tile
    for q in range(4):
        for t in range(8):
            mine = pl.multiple_of((4 * h + q) * SHARD + 1024 + 32 * t, 32)
            theirs = pl.multiple_of((4 * (1 - h) + q) * SHARD + 1024 + 32 * t, 32)
            part[pl.ds(mine, 32), :] = keep[q, :, 128 * t : 128 * t + 128]
            part[pl.ds(theirs, 32), :] = recv[q, :, 128 * t : 128 * t + 128]
    leaving.wait()


def backward(act, slope, probs, pslope, normed, datt, dhu, stats, keep, recv):
    return pl.pallas_call(
        backward_kernel,
        out_shape=[shape((8 * SHARD, 128), BF), shape((L, D), BF)],
        in_specs=[ANY] * 5 + [VM] * 5,
        out_specs=[VM, ANY],
        scratch_shapes=[
            pltpu.VMEM((L, D), BF),
            pltpu.VMEM((L, D), BF),
            pltpu.VMEM((L, L), BF),
            pltpu.VMEM((L, L), BF),
            pltpu.VMEM((L, D), BF),
            pltpu.VMEM((L, D), BF),
            pltpu.VMEM((L, L), BF),
            pltpu.VMEM((L, 256), BF),
            pltpu.SemaphoreType.DMA((6,)),
        ],
        compiler_params=params(34),
        name="backward",
    )(act, slope, probs, pslope, normed, datt, dhu, stats, keep, recv)


def input_kernel(dhid, normed, stats, wag, own, other, w, sem):
    h = lax.axis_index("core")
    run_copies(load_weights(wag, w, sem, 0))
    for i in range(NQ):
        at = pl.ds(i * BQ, BQ)
        dn = nt(dhid[at, :], w[...])
        n = normed[at, :].astype(F32)
        r = stats[at, 4:5]
        mean = jnp.mean(dn, axis=-1, keepdims=True)
        cross = jnp.mean(dn * n, axis=-1, keepdims=True)
        res = (r * (dn - mean - n * cross)).astype(BF)
        to = pl.ds((i % 2) * BQ, BQ)

        @pl.when(h == i // 2)
        def _(res=res, to=to):
            own[to, :] = res

        @pl.when(h != i // 2)
        def _(res=res, to=to):
            other[to, :] = res


def input_grad(dhid, normed, stats, wag):
    return pl.pallas_call(
        input_kernel,
        out_shape=[shape((512, D), BF)] * 2,
        in_specs=[VM] * 3 + [ANY],
        out_specs=[VM, VM],
        scratch_shapes=[pltpu.VMEM((D, D), BF), pltpu.SemaphoreType.DMA((8,))],
        compiler_params=params(20),
        name="input_grad",
    )(dhid, normed, stats, wag)


def add_kernel(a, b, *outs):
    _, p, _ = unit_of()
    for k in range(4):
        at = rows(jnp.bitwise_xor(p, k) * 128, 128)
        outs[k][...] = (a[at, :].astype(F32) + b[at, :].astype(F32)).astype(BF)


def add_halves(a, b):
    return pl.pallas_call(
        add_kernel,
        out_shape=[shape((128, D), BF)] * 4,
        in_specs=[VM, VM],
        out_specs=[VM] * 4,
        compiler_params=params(16),
        name="add_halves",
    )(a, b)


def place_kernel(*refs):
    chunks, out, sem = refs[:4], refs[4], refs[5]
    run_copies(
        [
            pltpu.make_async_copy(chunks[k], out.at[jnp.bitwise_xor(lax.axis_index("x"), k)], sem.at[k])
            for k in range(4)
        ]
    )


def place(chunks):
    return pl.pallas_call(
        place_kernel,
        out_shape=shape((4, 128, D), BF),
        in_specs=[ANY] * 4,
        out_specs=VM,
        scratch_shapes=[pltpu.SemaphoreType.DMA((4,))],
        compiler_params=params(16),
        name="place",
    )(*chunks)


def finish_kernel(mine, theirs, w_in, w_out, bias):
    for core in range(2):

        @pl.when(lax.axis_index("core") == core)
        def _(core=core):
            for side, src in ((core, mine), (1 - core, theirs)):
                for t in range(8):
                    col = 512 * (t // 2) + 256 * side + 128 * (t % 2)
                    w_in[:, col : col + 128] = src[128 * t : 128 * t + 128, :].astype(F32) / 128.0
                    at = 1024 + 32 * t
                    row, col = 32 * (t // 4), 512 * side + 128 * (t % 4)
                    w_out[row : row + 32, col : col + 128] = (
                        src[at : at + 32, :].astype(F32) / 128.0
                    )
                tail = src[1280:1296, :].astype(F32)
                bias[side : side + 1, :] = (tail[0:1] + tail[1:2]) / 128.0


def finish(mine, theirs):
    return pl.pallas_call(
        finish_kernel,
        out_shape=[shape((128, 2 * D), F32), shape((64, D), F32), shape((2, 128), F32)],
        in_specs=[VM, VM],
        out_specs=[VM] * 3,
        compiler_params=params(16),
        name="finish",
    )(mine, theirs)


def device(yh, core, yl, x):
    return ((yh * 2 + core) * 2 + yl) * 4 + x


def unit_device(e, p, half):
    ye, ce = e >> 1, e & 1
    yp, cp = p >> 1, p & 1
    return device(ye, half, yp, 2 * (ye ^ cp) + ce)


def input_pairs(k):
    pairs = []
    for p in range(4):
        for yl in range(2):
            for x in range(4):
                pairs.append((device(p >> 1, p & 1, yl, x), unit_device(x ^ k, p, yl)))
    return pairs


def grad_pairs(k):
    pairs = []
    for e in range(4):
        for yl in range(2):
            for x in range(4):
                pairs.append((device(e >> 1, e & 1, yl, x), unit_device(e, x ^ k, yl)))
    return pairs


def back_pairs(k):
    return [(b, a) for a, b in grad_pairs(k)]


def local(layer_in, repack_plan, lengths, stamps, w_in, w_out, time_bias, grad_out):
    first = lax.axis_index("core") == 0
    swap = functools.partial(lax.ppermute, axis_name="core", perm=[(0, 1), (1, 0)])

    *chunks, wsel = prepare(repack_plan, layer_in, w_in, w_out)
    wag = lax.all_gather(wsel, "z", axis=0, tiled=True)
    xs = [lax.ppermute(c, PLANE, input_pairs(k)) for k, c in enumerate(chunks)]
    picked = pick(lengths, grad_out, stamps)
    gs = [lax.ppermute(c, PLANE, grad_pairs(k)) for k, c in enumerate(picked)]
    xs = xs + [swap(c) for c in xs]
    gs = gs + [swap(c) for c in gs]
    w3 = wag.reshape(8, 160, D)
    wrecv = swap(jnp.where(first, w3[4:, 128:], w3[:4, 128:]))

    normed, act, slope, probs, pslope, mixed, dz, stats = forward(time_bias, xs, gs, wag, wrecv)
    datt, dhu, keep, send = middle(stats, swap(stats), mixed, dz, act, slope, gs)
    part, dhid = backward(
        act, slope, probs, pslope, normed, datt, dhu, stats, keep, swap(send)
    )
    mine = lax.psum_scatter(part, "z", scatter_dimension=0, tiled=True)
    own, other = input_grad(dhid, normed, stats, wag)
    pieces = add_halves(own, swap(other))
    back = [lax.ppermute(pieces[k], PLANE, back_pairs(k)) for k in range(4)]
    input_gradient = place(back)
    mine, input_gradient = lax.optimization_barrier((mine, input_gradient))

    def exchange(v):
        return lax.all_to_all(v, CHIPS, split_axis=0, concat_axis=0, tiled=True)

    spread = exchange(mine.reshape(16, SHARD // 16, 128))
    summed = jnp.sum(spread.astype(F32), axis=0, keepdims=True).astype(BF)
    mine = exchange(jnp.broadcast_to(summed, spread.shape)).reshape(SHARD, 128)
    grad_w_in, grad_w_out, grad_bias = finish(mine, swap(mine))
    return input_gradient, grad_w_in, grad_w_out, grad_bias


def solution(mesh):
    fine = Mesh(mesh.devices.reshape(2, 2, 2, 4, 8), ("yh", "core", "yl", "x", "z"))
    events = P(("yh", "core", "z"), ("yl", "x"), None)
    slots = P(("yh", "core", "z"))
    return jax.shard_map(
        local,
        mesh=fine,
        in_specs=(
            events,
            slots,
            slots,
            P(("yh", "core", "z"), ("yl", "x")),
            P("z", None),
            P("z", None),
            P(),
            events,
        ),
        out_specs=(events, P("z", None), P("z", None), P()),
        check_vma=False,
    )
```

```python
import functools

import jax
import jax.numpy as jnp
from jax import lax
from jax.experimental import pallas as pl
from jax.experimental.pallas import tpu as pltpu
from jax.sharding import Mesh
from jax.sharding import PartitionSpec as P

DH = 256
D = 1024
L = 1024
EPS = 1e-05
BF = jnp.bfloat16
F32 = jnp.float32
BQ = 256
NQ = L // BQ
SHARD = 1408
PLANE = ("yh", "core", "yl", "x")
CHIPS = ("yh", "yl", "x")
ANY = pl.BlockSpec(memory_space=pl.ANY)
VM = pl.BlockSpec(memory_space=pltpu.VMEM)
SM = pl.BlockSpec(memory_space=pltpu.SMEM)
HB = pl.BlockSpec(memory_space=pltpu.HBM)


def params(mib):
    return pltpu.CompilerParams(vmem_limit_bytes=mib << 20)


def shape(dims, kind):
    return jax.ShapeDtypeStruct(dims, kind)


def nn(a, b):
    return lax.dot_general(a, b, (((1,), (0,)), ((), ())), preferred_element_type=F32)


def nt(a, b):
    return lax.dot_general(a, b, (((1,), (1,)), ((), ())), preferred_element_type=F32)


def tn(a, b):
    return lax.dot_general(a, b, (((0,), (0,)), ((), ())), preferred_element_type=F32)


def rows(start, size):
    return pl.ds(pl.multiple_of(start, size), size)


def run_copies(copies):
    for c in copies:
        c.start()
    for c in copies:
        c.wait()


def unit_of():
    yh, core, yl, x = (lax.axis_index(n) for n in PLANE)
    e = 2 * yh + jnp.bitwise_and(x, 1)
    p = 2 * yl + jnp.bitwise_xor(lax.shift_right_logical(x, 1), yh)
    return e, p, core


def weights_kernel(w_in, w_out, wsel, sem):
    h = lax.axis_index("core")
    copies = [
        pltpu.make_async_copy(
            w_in.at[:, rows(512 * c + 256 * h, 256)],
            wsel.at[pl.ds(0, 128), pl.ds(256 * c, 256)],
            sem.at[c],
        )
        for c in range(4)
    ] + [
        pltpu.make_async_copy(
            w_out.at[pl.ds(32 * r, 32), rows(512 * h, 512)],
            wsel.at[pl.ds(128, 32), pl.ds(512 * r, 512)],
            sem.at[4 + r],
        )
        for r in range(2)
    ]
    run_copies(copies)


def own_weights(w_in, w_out):
    return pl.pallas_call(
        weights_kernel,
        out_shape=shape((160, D), BF),
        in_specs=[HB, HB],
        out_specs=VM,
        scratch_shapes=[pltpu.SemaphoreType.DMA((6,))],
        compiler_params=params(60),
        name="own_weights",
    )(w_in, w_out)


def deal_kernel(plan, lay, *refs):
    outs, sem = refs[:4], refs[4]
    x = lax.axis_index("x")
    run_copies(
        [
            pltpu.make_async_copy(lay.at[plan[jnp.bitwise_xor(x, k)]], outs[k], sem.at[k])
            for k in range(4)
        ]
    )


def deal(plan, lay):
    return pl.pallas_call(
        deal_kernel,
        out_shape=[shape((128, D), BF)] * 4,
        in_specs=[SM, HB],
        out_specs=[VM] * 4,
        scratch_shapes=[pltpu.SemaphoreType.DMA((4,))],
        compiler_params=params(60),
        name="deal",
    )(plan, lay)


def pick_kernel(lengths, grad, stamps, *refs):
    outs, sem = refs[:4], refs[4]
    slots = [jnp.bitwise_xor(lax.axis_index("x"), k) for k in range(4)]
    copies = [
        pltpu.make_async_copy(grad.at[slots[k]], outs[k].at[pl.ds(0, 128)], sem.at[k])
        for k in range(4)
    ]
    for c in copies:
        c.start()
    here = (lax.axis_index("yl") * 4 + lax.axis_index("x")) * 128 + lax.broadcasted_iota(jnp.int32, (16, 128), 1)
    line = lax.broadcasted_iota(jnp.int32, (16, 128), 0)
    for k in range(4):
        time = jnp.broadcast_to(stamps[pl.ds(slots[k], 1), :].astype(F32), (16, 128))
        alive = jnp.where(here < lengths[slots[k]], 1.0, 0.0)
        value = jnp.where(line == 0, time, jnp.where(line == 1, alive, 0.0))
        outs[k][128:144, 0:128] = value.astype(BF)
        outs[k][128:144, 128:1024] = jnp.zeros((16, 896), BF)
    for c in copies:
        c.wait()


def pick(lengths, grad, stamps):
    return pl.pallas_call(
        pick_kernel,
        out_shape=[shape((144, D), BF)] * 4,
        in_specs=[SM, HB, VM],
        out_specs=[VM] * 4,
        scratch_shapes=[pltpu.SemaphoreType.DMA((4,))],
        compiler_params=params(24),
        name="pick",
    )(lengths, grad, stamps)


def block_of(h, other, k):
    half = h if k < 4 else 1 - h
    return half * 4 + jnp.bitwise_xor(other, k % 4)


def load_grad(gs, grad, p, h, sem, first):
    return [
        pltpu.make_async_copy(
            gs[k].at[pl.ds(0, 128)],
            grad.at[rows(block_of(h, p, k) * 128, 128)],
            sem.at[first + k],
        )
        for k in range(8)
    ]


def load_weights(wag, w, sem, first):
    return [
        pltpu.make_async_copy(
            wag.at[pl.ds(160 * z, 128)], w.at[pl.ds(128 * z, 128)], sem.at[first + z]
        )
        for z in range(8)
    ]


def forward_kernel(tb, *refs):
    xs, gs, wag = refs[:8], refs[8:16], refs[16]
    nv, av, sv, pv, qv, mixed, stats = refs[17:24]
    x, w, small, scol, srow, sem = refs[24:]
    e, p, h = unit_of()
    copies = load_weights(wag, w, sem, 0)
    for k in range(8):
        copies.append(
            pltpu.make_async_copy(
                xs[k], x.at[rows(block_of(h, e, k) * 128, 128)], sem.at[8 + k]
            )
        )
        copies.append(
            pltpu.make_async_copy(
                gs[k].at[pl.ds(128, 16), pl.ds(0, 128)],
                small.at[block_of(h, p, k)],
                sem.at[16 + k],
            )
        )
    run_copies(copies)

    for i in range(NQ):
        at = pl.ds(i * BQ, BQ)
        v = x[at, :].astype(F32)
        v = v - jnp.mean(v, axis=-1, keepdims=True)
        r = lax.rsqrt(jnp.mean(v * v, axis=-1, keepdims=True) + EPS)
        n = (v * r).astype(BF)
        nv[at, :] = n
        stats[at, :] = jnp.broadcast_to(r, (BQ, 128))
        for c in range(4):
            cols = pl.ds(256 * c, 256)
            hidden = nn(n, w[:, cols])
            sg = jax.nn.sigmoid(hidden)
            av[at, cols] = (hidden * sg).astype(BF)
            sv[at, cols] = (sg * (1.0 + hidden * (1.0 - sg))).astype(BF)

    for b in range(8):
        tile = small[b].astype(F32)
        srow[0:8, pl.ds(128 * b, 128)] = tile[0:8]
        full = jnp.concatenate([tile, jnp.zeros((112, 128), F32)], axis=0)
        scol[pl.ds(128 * b, 128), :] = jnp.transpose(full)

    both = tb[...].astype(F32)
    table = jnp.broadcast_to(jnp.where(h == 0, both[0:1], both[1:2]), (BQ, 128))
    lane = lax.broadcasted_iota(jnp.int32, (BQ, 128), 1)
    causal = (
        lax.broadcasted_iota(jnp.int32, (BQ, BQ), 1)
        <= lax.broadcasted_iota(jnp.int32, (BQ, BQ), 0)
    )
    for i in range(NQ):
        at = pl.ds(i * BQ, BQ)
        q = (av[at, 512:768].astype(F32) * (DH**-0.5)).astype(BF)
        si = scol[at, 0:1]
        lv = scol[at, 1:2]
        for j in range(i + 1):
            cols = pl.ds(j * BQ, BQ)
            s = nt(q, av[cols, 768:1024])
            near = jnp.clip(si - srow[0:1, cols], 0.0, 127.0).astype(jnp.int32)
            bias = jnp.concatenate(
                [
                    jnp.take_along_axis(table, near[:, :128], axis=1, mode="promise_in_bounds"),
                    jnp.take_along_axis(table, near[:, 128:], axis=1, mode="promise_in_bounds"),
                ],
                axis=1,
            )
            s = s + bias
            sg = jax.nn.sigmoid(s)
            live = jnp.where(causal, lv, 0.0) if j == i else lv
            pv[at, cols] = (s * sg * live).astype(BF)
            qv[at, cols] = (sg * (1.0 + s * (1.0 - sg)) * live).astype(BF)
        upto = (i + 1) * BQ
        mixed[at, :] = nn(pv[at, 0:upto], av[0:upto, 256:512])
        stats[at, :] = jnp.where(lane == 5, si, stats[at, :])


def forward(tb, xs, gs, wag):
    return pl.pallas_call(
        forward_kernel,
        out_shape=[shape((L, D), BF)] * 3
        + [shape((L, L), BF)] * 2
        + [shape((L, DH), F32), shape((L, 128), F32)],
        in_specs=[VM] + [HB] * 17,
        out_specs=[VM] * 7,
        scratch_shapes=[
            pltpu.VMEM((L, D), BF),
            pltpu.VMEM((D, D), BF),
            pltpu.VMEM((8, 16, 128), BF),
            pltpu.VMEM((L, 128), F32),
            pltpu.VMEM((8, L), F32),
            pltpu.SemaphoreType.DMA((24,)),
        ],
        compiler_params=params(28),
        name="forward",
    )(tb, *xs, *gs, wag)


def statistics_kernel(mixed, gate, base, *refs):
    gs, wag, wrecv = refs[:8], refs[8], refs[9]
    dz, stats, grad, wo, sem = refs[10:]
    _, p, h = unit_of()
    copies = load_grad(gs, grad, p, h, sem, 0)
    for q in range(4):
        for r in range(2):
            own = wag.at[
                pl.ds(pl.multiple_of((4 * h + q) * 160 + 128, 32), 32), pl.ds(512 * r, 512)
            ]
            other = wrecv.at[q, :, pl.ds(512 * r, 512)]
            to = pl.ds(64 * q + 32 * r, 32)
            n = 8 + 4 * q + 2 * r
            copies.append(pltpu.make_async_copy(own, wo.at[to, rows(h * 512, 512)], sem.at[n]))
            copies.append(
                pltpu.make_async_copy(other, wo.at[to, rows((1 - h) * 512, 512)], sem.at[n + 1])
            )
    run_copies(copies)
    lane = lax.broadcasted_iota(jnp.int32, (BQ, 128), 1)
    for i in range(NQ):
        at = pl.ds(i * BQ, BQ)
        d = nt(grad[at, :], wo[...])
        dz[at, :] = d
        gated = mixed[at, :] * gate[at, 0:256].astype(F32)
        m = jnp.mean(gated, axis=-1, keepdims=True)
        centred = gated - m
        m2 = jnp.sum(centred * centred, axis=-1, keepdims=True)
        s3 = jnp.sum(d, axis=-1, keepdims=True)
        s4 = jnp.sum(d * centred, axis=-1, keepdims=True)
        row = base[at, :]
        for n, value in enumerate((m, m2, s3, s4)):
            row = jnp.where(lane == n, value, row)
        stats[at, :] = row


def statistics(mixed, act, base, gs, wag, wrecv):
    return pl.pallas_call(
        statistics_kernel,
        out_shape=[shape((L, DH), F32), shape((L, 128), F32)],
        in_specs=[VM, VM, VM] + [HB] * 10,
        out_specs=[VM, VM],
        scratch_shapes=[
            pltpu.VMEM((L, D), BF),
            pltpu.VMEM((DH, D), BF),
            pltpu.SemaphoreType.DMA((24,)),
        ],
        compiler_params=params(16),
        name="statistics",
    )(mixed, act, base, *gs, wag, wrecv)


def middle_kernel(own, peer, mixed, dz, gate, gslope, *refs):
    gs = refs[:8]
    datt, dhu, keep, send, zl, grad, sem = refs[8:]
    _, p, h = unit_of()
    copies = load_grad(gs, grad, p, h, sem, 0)
    for c in copies:
        c.start()
    for i in range(NQ):
        at = pl.ds(i * BQ, BQ)
        a, b = own[at, :], peer[at, :]
        m0, m1 = a[:, 0:1], b[:, 0:1]
        mean = 0.5 * (m0 + m1)
        gap = m0 - mean
        r = lax.rsqrt((a[:, 1:2] + b[:, 1:2] + 512.0 * gap * gap) * (1.0 / 512.0) + EPS)
        dmean = (a[:, 2:3] + b[:, 2:3]) * (1.0 / 512.0)
        cross = a[:, 3:4] + b[:, 3:4] + gap * (a[:, 2:3] - b[:, 2:3])
        cross = cross * r * (1.0 / 512.0)
        mix = mixed[at, :]
        u = gate[at, 0:256].astype(F32)
        zhat = (mix * u - mean) * r
        zl[at, :] = zhat.astype(BF)
        dgated = r * (dz[at, :] - dmean - zhat * cross)
        datt[at, :] = (dgated * u).astype(BF)
        dhu[at, :] = (dgated * mix * gslope[at, 0:256].astype(F32)).astype(BF)
    for c in copies:
        c.wait()
    out = tn(zl[...], grad[...]).astype(BF)
    for half in range(2):
        for q in range(4):
            block = jnp.concatenate(
                [
                    out[64 * q + r : 64 * q + r + 32, 512 * half : 512 * half + 512]
                    for r in (0, 32)
                ],
                axis=1,
            )

            @pl.when(h == half)
            def _(block=block, q=q):
                keep[q] = block

            @pl.when(h != half)
            def _(block=block, q=q):
                send[q] = block


def middle(own, peer, mixed, dz, act, slope, gs):
    return pl.pallas_call(
        middle_kernel,
        out_shape=[shape((L, DH), BF)] * 2 + [shape((4, 32, D), BF)] * 2,
        in_specs=[VM] * 6 + [HB] * 8,
        out_specs=[VM] * 4,
        scratch_shapes=[
            pltpu.VMEM((L, DH), BF),
            pltpu.VMEM((L, D), BF),
            pltpu.SemaphoreType.DMA((8,)),
        ],
        compiler_params=params(20),
        name="middle",
    )(own, peer, mixed, dz, act, slope, *gs)


def backward_kernel(
    act, slope, probs, pslope, normed, datt, dhu, stats, keep, recv, *refs
):
    part_out, dhid_out, part, dhid, dlow, hot, sem = refs
    h = lax.axis_index("core")
    stamp_lane = lax.broadcasted_iota(jnp.int32, (L, 256), 1).astype(F32)
    hot[...] = jnp.where(stats[:, 5:6] == stamp_lane, 1.0, 0.0).astype(BF)
    dhid[:, 0:256] = dhu[...]
    bucket = lax.broadcasted_iota(jnp.int32, (BQ, 128), 1)
    time = lax.broadcasted_iota(jnp.int32, (BQ, 256), 1)
    total = jnp.zeros((BQ, 128), F32)
    for i in range(NQ):
        at = pl.ds(i * BQ, BQ)
        upto = (i + 1) * BQ
        da = datt[at, :]
        for j in range(i + 1):
            cols = pl.ds(j * BQ, BQ)
            dp = nt(da, act[cols, 256:512])
            dlow[at, cols] = (dp * pslope[at, cols].astype(F32)).astype(BF)
        low = dlow[at, 0:upto]
        dq = nn(low, act[0:upto, 768:1024]) * (DH**-0.5)
        dhid[at, 512:768] = (dq * slope[at, 512:768].astype(F32)).astype(BF)
        by_time = nn(low, hot[0:upto, :])
        si = stats[at, 5:6].astype(jnp.int32)
        when = si - bucket
        index = jnp.bitwise_and(when, 127)
        early = jnp.take_along_axis(by_time[:, :128], index, axis=1, mode="promise_in_bounds")
        late = jnp.take_along_axis(by_time[:, 128:], index, axis=1, mode="promise_in_bounds")
        picked = jnp.where(when >= 128, late, jnp.where(when >= 0, early, 0.0))
        far = jnp.sum(jnp.where(time <= si - 127, by_time, 0.0), axis=-1, keepdims=True)
        total = total + jnp.where(bucket == 127, far, picked)
    for j in range(NQ):
        cols = pl.ds(j * BQ, BQ)
        frm = j * BQ
        dv = tn(probs[frm:, cols], datt[frm:, :])
        dhid[cols, 256:512] = (dv * slope[cols, 256:512].astype(F32)).astype(BF)
        dk = tn(dlow[frm:, cols], act[frm:, 512:768]) * (DH**-0.5)
        dhid[cols, 768:1024] = (dk * slope[cols, 768:1024].astype(F32)).astype(BF)
    leaving = [pltpu.make_async_copy(dhid, dhid_out, sem.at[4])]
    leaving[0].start()
    bias = jnp.sum(total, axis=0, keepdims=True)
    high = bias.astype(BF).astype(F32)
    line = lax.broadcasted_iota(jnp.int32, (128, 128), 0)
    tile = jnp.where(line == 0, high, jnp.where(line == 1, bias - high, 0.0)).astype(BF)
    for z in range(8):
        part[pl.ds(z * SHARD + 1280, 128), :] = tile
    for q in range(4):
        for t in range(8):
            mine = pl.multiple_of((4 * h + q) * SHARD + 1024 + 32 * t, 32)
            theirs = pl.multiple_of((4 * (1 - h) + q) * SHARD + 1024 + 32 * t, 32)
            part[pl.ds(mine, 32), :] = keep[q, :, 128 * t : 128 * t + 128]
            part[pl.ds(theirs, 32), :] = recv[q, :, 128 * t : 128 * t + 128]
    for b in range(4):
        pin = tn(normed[:, 256 * b : 256 * b + 256], dhid[...]).astype(BF)
        for z in range(2):
            for t in range(8):
                part[pl.ds((2 * b + z) * SHARD + 128 * t, 128), :] = pin[
                    128 * z : 128 * z + 128, 128 * t : 128 * t + 128
                ]
        two = pl.ds(2 * b * SHARD, 2 * SHARD)
        leaving.append(pltpu.make_async_copy(part.at[two], part_out.at[two], sem.at[b]))
        leaving[-1].start()
    for c in leaving:
        c.wait()


def backward(act, slope, probs, pslope, normed, datt, dhu, stats, keep, recv):
    return pl.pallas_call(
        backward_kernel,
        out_shape=[shape((8 * SHARD, 128), BF), shape((L, D), BF)],
        in_specs=[VM] * 10,
        out_specs=[HB, HB],
        scratch_shapes=[
            pltpu.VMEM((8 * SHARD, 128), BF),
            pltpu.VMEM((L, D), BF),
            pltpu.VMEM((L, L), BF),
            pltpu.VMEM((L, 256), BF),
            pltpu.SemaphoreType.DMA((5,)),
        ],
        compiler_params=params(28),
        name="backward",
    )(act, slope, probs, pslope, normed, datt, dhu, stats, keep, recv)


def input_kernel(dhid_in, normed_in, stats, wag, own, other, dhid, normed, w, sem):
    h = lax.axis_index("core")
    copies = load_weights(wag, w, sem, 0)
    blocks = []
    for i in range(NQ):
        at = pl.ds(i * BQ, BQ)
        blocks.append(
            [
                pltpu.make_async_copy(dhid_in.at[at], dhid.at[at], sem.at[8 + 2 * i]),
                pltpu.make_async_copy(normed_in.at[at], normed.at[at], sem.at[9 + 2 * i]),
            ]
        )
    for c in copies + sum(blocks, []):
        c.start()
    for c in copies:
        c.wait()
    for i in range(NQ):
        at = pl.ds(i * BQ, BQ)
        for c in blocks[i]:
            c.wait()
        dn = nt(dhid[at, :], w[...])
        n = normed[at, :].astype(F32)
        r = stats[at, 4:5]
        mean = jnp.mean(dn, axis=-1, keepdims=True)
        cross = jnp.mean(dn * n, axis=-1, keepdims=True)
        res = (r * (dn - mean - n * cross)).astype(BF)
        to = pl.ds((i % 2) * BQ, BQ)

        @pl.when(h == i // 2)
        def _(res=res, to=to):
            own[to, :] = res

        @pl.when(h != i // 2)
        def _(res=res, to=to):
            other[to, :] = res


def input_grad(dhid, normed, stats, wag):
    return pl.pallas_call(
        input_kernel,
        out_shape=[shape((512, D), BF)] * 2,
        in_specs=[HB, ANY, VM, HB],
        out_specs=[VM, VM],
        scratch_shapes=[
            pltpu.VMEM((L, D), BF),
            pltpu.VMEM((L, D), BF),
            pltpu.VMEM((D, D), BF),
            pltpu.SemaphoreType.DMA((16,)),
        ],
        compiler_params=params(20),
        name="input_grad",
    )(dhid, normed, stats, wag)


def add_kernel(a, b, *outs):
    _, p, _ = unit_of()
    for k in range(4):
        at = rows(jnp.bitwise_xor(p, k) * 128, 128)
        outs[k][...] = (a[at, :].astype(F32) + b[at, :].astype(F32)).astype(BF)


def add_halves(a, b):
    return pl.pallas_call(
        add_kernel,
        out_shape=[shape((128, D), BF)] * 4,
        in_specs=[VM, VM],
        out_specs=[VM] * 4,
        compiler_params=params(16),
        name="add_halves",
    )(a, b)


def place_kernel(*refs):
    chunks, out, sem = refs[:4], refs[4], refs[5]
    run_copies(
        [
            pltpu.make_async_copy(chunks[k], out.at[jnp.bitwise_xor(lax.axis_index("x"), k)], sem.at[k])
            for k in range(4)
        ]
    )


def place(chunks):
    return pl.pallas_call(
        place_kernel,
        out_shape=shape((4, 128, D), BF),
        in_specs=[ANY] * 4,
        out_specs=VM,
        scratch_shapes=[pltpu.SemaphoreType.DMA((4,))],
        compiler_params=params(16),
        name="place",
    )(*chunks)


def finish_kernel(mine, theirs, w_in, w_out, bias):
    for core in range(2):

        @pl.when(lax.axis_index("core") == core)
        def _(core=core):
            for side, src in ((core, mine), (1 - core, theirs)):
                for t in range(8):
                    col = 512 * (t // 2) + 256 * side + 128 * (t % 2)
                    w_in[:, col : col + 128] = src[128 * t : 128 * t + 128, :].astype(F32) / 128.0
                    at = 1024 + 32 * t
                    row, col = 32 * (t // 4), 512 * side + 128 * (t % 4)
                    w_out[row : row + 32, col : col + 128] = (
                        src[at : at + 32, :].astype(F32) / 128.0
                    )
                tail = src[1280:1296, :].astype(F32)
                bias[side : side + 1, :] = (tail[0:1] + tail[1:2]) / 128.0


def finish(mine, theirs):
    return pl.pallas_call(
        finish_kernel,
        out_shape=[shape((128, 2 * D), F32), shape((64, D), F32), shape((2, 128), F32)],
        in_specs=[VM, VM],
        out_specs=[VM] * 3,
        compiler_params=params(16),
        name="finish",
    )(mine, theirs)


def device(yh, core, yl, x):
    return ((yh * 2 + core) * 2 + yl) * 4 + x


def unit_device(e, p, half):
    ye, ce = e >> 1, e & 1
    yp, cp = p >> 1, p & 1
    return device(ye, half, yp, 2 * (ye ^ cp) + ce)


def input_pairs(k):
    pairs = []
    for p in range(4):
        for yl in range(2):
            for x in range(4):
                pairs.append((device(p >> 1, p & 1, yl, x), unit_device(x ^ k, p, yl)))
    return pairs


def grad_pairs(k):
    pairs = []
    for e in range(4):
        for yl in range(2):
            for x in range(4):
                pairs.append((device(e >> 1, e & 1, yl, x), unit_device(e, x ^ k, yl)))
    return pairs


def back_pairs(k):
    return [(b, a) for a, b in grad_pairs(k)]


def local(layer_in, repack_plan, lengths, stamps, w_in, w_out, time_bias, grad_out):
    first = lax.axis_index("core") == 0
    swap = functools.partial(lax.ppermute, axis_name="core", perm=[(0, 1), (1, 0)])

    wag = lax.all_gather(own_weights(w_in, w_out), "z", axis=0, tiled=True)
    chunks = deal(repack_plan, layer_in)
    xs = [lax.ppermute(c, PLANE, input_pairs(k)) for k, c in enumerate(chunks)]
    picked = pick(lengths, grad_out, stamps)
    gs = [lax.ppermute(c, PLANE, grad_pairs(k)) for k, c in enumerate(picked)]
    xs = xs + [swap(c) for c in xs]
    gs = gs + [swap(c) for c in gs]
    w3 = wag.reshape(8, 160, D)
    wrecv = swap(jnp.where(first, w3[4:, 128:], w3[:4, 128:]))

    normed, act, slope, probs, pslope, mixed, base = forward(time_bias, xs, gs, wag)
    dz, stats = statistics(mixed, act, base, gs, wag, wrecv)
    datt, dhu, keep, send = middle(stats, swap(stats), mixed, dz, act, slope, gs)
    part, dhid = backward(
        act, slope, probs, pslope, normed, datt, dhu, stats, keep, swap(send)
    )
    mine = lax.psum_scatter(part, "z", scatter_dimension=0, tiled=True)
    own, other = input_grad(dhid, normed, stats, wag)
    pieces = add_halves(own, swap(other))
    back = [lax.ppermute(pieces[k], PLANE, back_pairs(k)) for k in range(4)]
    input_gradient = place(back)
    mine, input_gradient = lax.optimization_barrier((mine, input_gradient))

    def exchange(v):
        return lax.all_to_all(v, CHIPS, split_axis=0, concat_axis=0, tiled=True)

    spread = exchange(mine.reshape(16, SHARD // 16, 128))
    summed = jnp.sum(spread.astype(F32), axis=0, keepdims=True).astype(BF)
    mine = exchange(jnp.broadcast_to(summed, spread.shape)).reshape(SHARD, 128)
    grad_w_in, grad_w_out, grad_bias = finish(mine, swap(mine))
    return input_gradient, grad_w_in, grad_w_out, grad_bias


def solution(mesh):
    fine = Mesh(mesh.devices.reshape(2, 2, 2, 4, 8), ("yh", "core", "yl", "x", "z"))
    events = P(("yh", "core", "z"), ("yl", "x"), None)
    slots = P(("yh", "core", "z"))
    return jax.shard_map(
        local,
        mesh=fine,
        in_specs=(
            events,
            slots,
            slots,
            P(("yh", "core", "z"), ("yl", "x")),
            P("z", None),
            P("z", None),
            P(),
            events,
        ),
        out_specs=(events, P("z", None), P("z", None), P()),
        check_vma=False,
    )
```

```python
import functools

import jax
import jax.numpy as jnp
from jax import lax
from jax.experimental import pallas as pl
from jax.experimental.pallas import tpu as pltpu
from jax.sharding import Mesh
from jax.sharding import PartitionSpec as P

DH = 256
D = 1024
L = 1024
EPS = 1e-05
BF = jnp.bfloat16
F32 = jnp.float32
BQ = 256
NQ = L // BQ
SENT = 1296
SHARD = 1408
PLANE = ("yh", "core", "yl", "x")
CHIPS = ("yh", "yl", "x")
ANY = pl.BlockSpec(memory_space=pl.ANY)
VM = pl.BlockSpec(memory_space=pltpu.VMEM)
SM = pl.BlockSpec(memory_space=pltpu.SMEM)
HB = pl.BlockSpec(memory_space=pltpu.HBM)


def params(mib):
    return pltpu.CompilerParams(vmem_limit_bytes=mib << 20)


def shape(dims, kind):
    return jax.ShapeDtypeStruct(dims, kind)


def nn(a, b):
    return lax.dot_general(a, b, (((1,), (0,)), ((), ())), preferred_element_type=F32)


def nt(a, b):
    return lax.dot_general(a, b, (((1,), (1,)), ((), ())), preferred_element_type=F32)


def tn(a, b):
    return lax.dot_general(a, b, (((0,), (0,)), ((), ())), preferred_element_type=F32)


def rows(start, size):
    return pl.ds(pl.multiple_of(start, size), size)


def run_copies(copies):
    for c in copies:
        c.start()
    for c in copies:
        c.wait()


def unit_of():
    yh, core, yl, x = (lax.axis_index(n) for n in PLANE)
    e = 2 * yh + jnp.bitwise_and(x, 1)
    p = 2 * yl + jnp.bitwise_xor(lax.shift_right_logical(x, 1), yh)
    return e, p, core


def weights_kernel(w_in, w_out, wsel, sem):
    h = lax.axis_index("core")
    copies = [
        pltpu.make_async_copy(
            w_in.at[:, rows(512 * c + 256 * h, 256)],
            wsel.at[pl.ds(0, 128), pl.ds(256 * c, 256)],
            sem.at[c],
        )
        for c in range(4)
    ] + [
        pltpu.make_async_copy(
            w_out.at[pl.ds(32 * r, 32), rows(512 * h, 512)],
            wsel.at[pl.ds(128, 32), pl.ds(512 * r, 512)],
            sem.at[4 + r],
        )
        for r in range(2)
    ]
    run_copies(copies)


def own_weights(w_in, w_out):
    return pl.pallas_call(
        weights_kernel,
        out_shape=shape((160, D), BF),
        in_specs=[HB, HB],
        out_specs=VM,
        scratch_shapes=[pltpu.SemaphoreType.DMA((6,))],
        compiler_params=params(60),
        name="own_weights",
    )(w_in, w_out)


def deal_kernel(plan, lay, *refs):
    outs, sem = refs[:4], refs[4]
    x = lax.axis_index("x")
    run_copies(
        [
            pltpu.make_async_copy(lay.at[plan[jnp.bitwise_xor(x, k)]], outs[k], sem.at[k])
            for k in range(4)
        ]
    )


def deal(plan, lay):
    return pl.pallas_call(
        deal_kernel,
        out_shape=[shape((128, D), BF)] * 4,
        in_specs=[SM, HB],
        out_specs=[VM] * 4,
        scratch_shapes=[pltpu.SemaphoreType.DMA((4,))],
        compiler_params=params(60),
        name="deal",
    )(plan, lay)


def pick_kernel(lengths, grad, stamps, *refs):
    outs, sem = refs[:4], refs[4]
    slots = [jnp.bitwise_xor(lax.axis_index("x"), k) for k in range(4)]
    copies = [
        pltpu.make_async_copy(grad.at[slots[k]], outs[k].at[pl.ds(0, 128)], sem.at[k])
        for k in range(4)
    ]
    for c in copies:
        c.start()
    here = (lax.axis_index("yl") * 4 + lax.axis_index("x")) * 128 + lax.broadcasted_iota(jnp.int32, (16, 128), 1)
    line = lax.broadcasted_iota(jnp.int32, (16, 128), 0)
    for k in range(4):
        time = jnp.broadcast_to(stamps[pl.ds(slots[k], 1), :].astype(F32), (16, 128))
        alive = jnp.where(here < lengths[slots[k]], 1.0, 0.0)
        value = jnp.where(line == 0, time, jnp.where(line == 1, alive, 0.0))
        outs[k][128:144, 0:128] = value.astype(BF)
        outs[k][128:144, 128:1024] = jnp.zeros((16, 896), BF)
    for c in copies:
        c.wait()


def pick(lengths, grad, stamps):
    return pl.pallas_call(
        pick_kernel,
        out_shape=[shape((144, D), BF)] * 4,
        in_specs=[SM, HB, VM],
        out_specs=[VM] * 4,
        scratch_shapes=[pltpu.SemaphoreType.DMA((4,))],
        compiler_params=params(24),
        name="pick",
    )(lengths, grad, stamps)


def block_of(h, other, k):
    half = h if k < 4 else 1 - h
    return half * 4 + jnp.bitwise_xor(other, k % 4)


def load_grad(gs, grad, p, h, sem, first):
    return [
        pltpu.make_async_copy(
            gs[k].at[pl.ds(0, 128)],
            grad.at[rows(block_of(h, p, k) * 128, 128)],
            sem.at[first + k],
        )
        for k in range(8)
    ]


def load_weights(wag, w, sem, first):
    return [
        pltpu.make_async_copy(
            wag.at[pl.ds(160 * z, 128)], w.at[pl.ds(128 * z, 128)], sem.at[first + z]
        )
        for z in range(8)
    ]


def forward_kernel(tb, *refs):
    xs, gs, wag = refs[:8], refs[8:16], refs[16]
    nv, av, sv, pv, qv, mixed, stats = refs[17:24]
    x, w, small, scol, srow, sem = refs[24:]
    e, p, h = unit_of()
    copies = load_weights(wag, w, sem, 0)
    for k in range(8):
        copies.append(
            pltpu.make_async_copy(
                xs[k], x.at[rows(block_of(h, e, k) * 128, 128)], sem.at[8 + k]
            )
        )
        copies.append(
            pltpu.make_async_copy(
                gs[k].at[pl.ds(128, 16), pl.ds(0, 128)],
                small.at[block_of(h, p, k)],
                sem.at[16 + k],
            )
        )
    run_copies(copies)

    for i in range(NQ):
        at = pl.ds(i * BQ, BQ)
        v = x[at, :].astype(F32)
        v = v - jnp.mean(v, axis=-1, keepdims=True)
        r = lax.rsqrt(jnp.mean(v * v, axis=-1, keepdims=True) + EPS)
        n = (v * r).astype(BF)
        nv[at, :] = n
        stats[at, :] = jnp.broadcast_to(r, (BQ, 128))
        for c in range(4):
            cols = pl.ds(256 * c, 256)
            hidden = nn(n, w[:, cols])
            sg = jax.nn.sigmoid(hidden)
            av[at, cols] = (hidden * sg).astype(BF)
            sv[at, cols] = (sg * (1.0 + hidden * (1.0 - sg))).astype(BF)

    for b in range(8):
        tile = small[b].astype(F32)
        srow[0:8, pl.ds(128 * b, 128)] = tile[0:8]
        full = jnp.concatenate([tile, jnp.zeros((112, 128), F32)], axis=0)
        scol[pl.ds(128 * b, 128), :] = jnp.transpose(full)

    both = tb[...].astype(F32)
    table = jnp.broadcast_to(jnp.where(h == 0, both[0:1], both[1:2]), (BQ, 128))
    lane = lax.broadcasted_iota(jnp.int32, (BQ, 128), 1)
    causal = (
        lax.broadcasted_iota(jnp.int32, (BQ, BQ), 1)
        <= lax.broadcasted_iota(jnp.int32, (BQ, BQ), 0)
    )
    for i in range(NQ):
        at = pl.ds(i * BQ, BQ)
        q = (av[at, 512:768].astype(F32) * (DH**-0.5)).astype(BF)
        si = scol[at, 0:1]
        lv = scol[at, 1:2]
        for j in range(i + 1):
            cols = pl.ds(j * BQ, BQ)
            s = nt(q, av[cols, 768:1024])
            near = jnp.clip(si - srow[0:1, cols], 0.0, 127.0).astype(jnp.int32)
            bias = jnp.concatenate(
                [
                    jnp.take_along_axis(table, near[:, :128], axis=1, mode="promise_in_bounds"),
                    jnp.take_along_axis(table, near[:, 128:], axis=1, mode="promise_in_bounds"),
                ],
                axis=1,
            )
            s = s + bias
            sg = jax.nn.sigmoid(s)
            live = jnp.where(causal, lv, 0.0) if j == i else lv
            pv[at, cols] = (s * sg * live).astype(BF)
            qv[at, cols] = (sg * (1.0 + s * (1.0 - sg)) * live).astype(BF)
        upto = (i + 1) * BQ
        mixed[at, :] = nn(pv[at, 0:upto], av[0:upto, 256:512])
        stats[at, :] = jnp.where(lane == 5, si, stats[at, :])


def forward(tb, xs, gs, wag):
    return pl.pallas_call(
        forward_kernel,
        out_shape=[shape((L, D), BF)] * 3
        + [shape((L, L), BF)] * 2
        + [shape((L, DH), F32), shape((L, 128), F32)],
        in_specs=[VM] + [HB] * 17,
        out_specs=[VM] * 7,
        scratch_shapes=[
            pltpu.VMEM((L, D), BF),
            pltpu.VMEM((D, D), BF),
            pltpu.VMEM((8, 16, 128), BF),
            pltpu.VMEM((L, 128), F32),
            pltpu.VMEM((8, L), F32),
            pltpu.SemaphoreType.DMA((24,)),
        ],
        compiler_params=params(28),
        name="forward",
    )(tb, *xs, *gs, wag)


def statistics_kernel(mixed, gate, base, *refs):
    gs, wag, wrecv = refs[:8], refs[8], refs[9]
    dz, stats, grad, wo, sem = refs[10:]
    _, p, h = unit_of()
    copies = load_grad(gs, grad, p, h, sem, 0)
    for q in range(4):
        for r in range(2):
            own = wag.at[
                pl.ds(pl.multiple_of((4 * h + q) * 160 + 128, 32), 32), pl.ds(512 * r, 512)
            ]
            other = wrecv.at[q, :, pl.ds(512 * r, 512)]
            to = pl.ds(64 * q + 32 * r, 32)
            n = 8 + 4 * q + 2 * r
            copies.append(pltpu.make_async_copy(own, wo.at[to, rows(h * 512, 512)], sem.at[n]))
            copies.append(
                pltpu.make_async_copy(other, wo.at[to, rows((1 - h) * 512, 512)], sem.at[n + 1])
            )
    run_copies(copies)
    lane = lax.broadcasted_iota(jnp.int32, (BQ, 128), 1)
    for i in range(NQ):
        at = pl.ds(i * BQ, BQ)
        d = nt(grad[at, :], wo[...])
        dz[at, :] = d
        gated = mixed[at, :] * gate[at, 0:256].astype(F32)
        m = jnp.mean(gated, axis=-1, keepdims=True)
        centred = gated - m
        m2 = jnp.sum(centred * centred, axis=-1, keepdims=True)
        s3 = jnp.sum(d, axis=-1, keepdims=True)
        s4 = jnp.sum(d * centred, axis=-1, keepdims=True)
        row = base[at, :]
        for n, value in enumerate((m, m2, s3, s4)):
            row = jnp.where(lane == n, value, row)
        stats[at, :] = row


def statistics(mixed, act, base, gs, wag, wrecv):
    return pl.pallas_call(
        statistics_kernel,
        out_shape=[shape((L, DH), F32), shape((L, 128), F32)],
        in_specs=[VM, VM, VM] + [HB] * 10,
        out_specs=[VM, VM],
        scratch_shapes=[
            pltpu.VMEM((L, D), BF),
            pltpu.VMEM((DH, D), BF),
            pltpu.SemaphoreType.DMA((24,)),
        ],
        compiler_params=params(16),
        name="statistics",
    )(mixed, act, base, *gs, wag, wrecv)


def middle_kernel(own, peer, mixed, dz, gate, gslope, *refs):
    gs = refs[:8]
    datt, dhu, keep, send, zl, grad, sem = refs[8:]
    _, p, h = unit_of()
    copies = load_grad(gs, grad, p, h, sem, 0)
    for c in copies:
        c.start()
    for i in range(NQ):
        at = pl.ds(i * BQ, BQ)
        a, b = own[at, :], peer[at, :]
        m0, m1 = a[:, 0:1], b[:, 0:1]
        mean = 0.5 * (m0 + m1)
        gap = m0 - mean
        r = lax.rsqrt((a[:, 1:2] + b[:, 1:2] + 512.0 * gap * gap) * (1.0 / 512.0) + EPS)
        dmean = (a[:, 2:3] + b[:, 2:3]) * (1.0 / 512.0)
        cross = a[:, 3:4] + b[:, 3:4] + gap * (a[:, 2:3] - b[:, 2:3])
        cross = cross * r * (1.0 / 512.0)
        mix = mixed[at, :]
        u = gate[at, 0:256].astype(F32)
        zhat = (mix * u - mean) * r
        zl[at, :] = zhat.astype(BF)
        dgated = r * (dz[at, :] - dmean - zhat * cross)
        datt[at, :] = (dgated * u).astype(BF)
        dhu[at, :] = (dgated * mix * gslope[at, 0:256].astype(F32)).astype(BF)
    for c in copies:
        c.wait()
    out = tn(zl[...], grad[...]).astype(BF)
    for half in range(2):
        for q in range(4):
            block = jnp.concatenate(
                [
                    out[64 * q + r : 64 * q + r + 32, 512 * half : 512 * half + 512]
                    for r in (0, 32)
                ],
                axis=1,
            )

            @pl.when(h == half)
            def _(block=block, q=q):
                keep[q] = block

            @pl.when(h != half)
            def _(block=block, q=q):
                send[q] = block


def middle(own, peer, mixed, dz, act, slope, gs):
    return pl.pallas_call(
        middle_kernel,
        out_shape=[shape((L, DH), BF)] * 2 + [shape((4, 32, D), BF)] * 2,
        in_specs=[VM] * 6 + [HB] * 8,
        out_specs=[VM] * 4,
        scratch_shapes=[
            pltpu.VMEM((L, DH), BF),
            pltpu.VMEM((L, D), BF),
            pltpu.SemaphoreType.DMA((8,)),
        ],
        compiler_params=params(20),
        name="middle",
    )(own, peer, mixed, dz, act, slope, *gs)


def backward_kernel(
    act, slope, probs, pslope, normed, datt, dhu, stats, keep, recv, *refs
):
    part_out, dhid_out, part, dhid, dlow, hot, sem = refs
    h = lax.axis_index("core")
    stamp_lane = lax.broadcasted_iota(jnp.int32, (L, 256), 1).astype(F32)
    hot[...] = jnp.where(stats[:, 5:6] == stamp_lane, 1.0, 0.0).astype(BF)
    dhid[:, 0:256] = dhu[...]
    bucket = lax.broadcasted_iota(jnp.int32, (BQ, 128), 1)
    time = lax.broadcasted_iota(jnp.int32, (BQ, 256), 1)
    total = jnp.zeros((BQ, 128), F32)
    for i in range(NQ):
        at = pl.ds(i * BQ, BQ)
        upto = (i + 1) * BQ
        da = datt[at, :]
        for j in range(i + 1):
            cols = pl.ds(j * BQ, BQ)
            dp = nt(da, act[cols, 256:512])
            dlow[at, cols] = (dp * pslope[at, cols].astype(F32)).astype(BF)
        low = dlow[at, 0:upto]
        dq = nn(low, act[0:upto, 768:1024]) * (DH**-0.5)
        dhid[at, 512:768] = (dq * slope[at, 512:768].astype(F32)).astype(BF)
        by_time = nn(low, hot[0:upto, :])
        si = stats[at, 5:6].astype(jnp.int32)
        when = si - bucket
        index = jnp.bitwise_and(when, 127)
        early = jnp.take_along_axis(by_time[:, :128], index, axis=1, mode="promise_in_bounds")
        late = jnp.take_along_axis(by_time[:, 128:], index, axis=1, mode="promise_in_bounds")
        picked = jnp.where(when >= 128, late, jnp.where(when >= 0, early, 0.0))
        far = jnp.sum(jnp.where(time <= si - 127, by_time, 0.0), axis=-1, keepdims=True)
        total = total + jnp.where(bucket == 127, far, picked)
    for j in range(NQ):
        cols = pl.ds(j * BQ, BQ)
        frm = j * BQ
        dv = tn(probs[frm:, cols], datt[frm:, :])
        dhid[cols, 256:512] = (dv * slope[cols, 256:512].astype(F32)).astype(BF)
        dk = tn(dlow[frm:, cols], act[frm:, 512:768]) * (DH**-0.5)
        dhid[cols, 768:1024] = (dk * slope[cols, 768:1024].astype(F32)).astype(BF)
    leaving = [pltpu.make_async_copy(dhid, dhid_out, sem.at[4])]
    leaving[0].start()
    bias = jnp.sum(total, axis=0, keepdims=True)
    high = bias.astype(BF).astype(F32)
    line = lax.broadcasted_iota(jnp.int32, (16, 128), 0)
    tile = jnp.where(line == 0, high, jnp.where(line == 1, bias - high, 0.0)).astype(BF)
    for z in range(8):
        part[pl.ds(z * SENT + 1280, 16), :] = tile
    for q in range(4):
        for t in range(8):
            mine = pl.multiple_of((4 * h + q) * SENT + 1024 + 32 * t, 16)
            theirs = pl.multiple_of((4 * (1 - h) + q) * SENT + 1024 + 32 * t, 16)
            part[pl.ds(mine, 32), :] = keep[q, :, 128 * t : 128 * t + 128]
            part[pl.ds(theirs, 32), :] = recv[q, :, 128 * t : 128 * t + 128]
    for b in range(4):
        pin = tn(normed[:, 256 * b : 256 * b + 256], dhid[...]).astype(BF)
        for z in range(2):
            for t in range(8):
                part[pl.ds((2 * b + z) * SENT + 128 * t, 128), :] = pin[
                    128 * z : 128 * z + 128, 128 * t : 128 * t + 128
                ]
        two = pl.ds(2 * b * SENT, 2 * SENT)
        leaving.append(pltpu.make_async_copy(part.at[two], part_out.at[two], sem.at[b]))
        leaving[-1].start()
    for c in leaving:
        c.wait()


def backward(act, slope, probs, pslope, normed, datt, dhu, stats, keep, recv):
    return pl.pallas_call(
        backward_kernel,
        out_shape=[shape((8 * SENT, 128), BF), shape((L, D), BF)],
        in_specs=[VM] * 10,
        out_specs=[HB, HB],
        scratch_shapes=[
            pltpu.VMEM((8 * SENT, 128), BF),
            pltpu.VMEM((L, D), BF),
            pltpu.VMEM((L, L), BF),
            pltpu.VMEM((L, 256), BF),
            pltpu.SemaphoreType.DMA((5,)),
        ],
        compiler_params=params(28),
        name="backward",
    )(act, slope, probs, pslope, normed, datt, dhu, stats, keep, recv)


def input_kernel(dhid_in, normed_in, stats, wag, own, other, dhid, normed, w, sem):
    h = lax.axis_index("core")
    copies = load_weights(wag, w, sem, 0)
    blocks = []
    for i in range(NQ):
        at = pl.ds(i * BQ, BQ)
        blocks.append(
            [
                pltpu.make_async_copy(dhid_in.at[at], dhid.at[at], sem.at[8 + 2 * i]),
                pltpu.make_async_copy(normed_in.at[at], normed.at[at], sem.at[9 + 2 * i]),
            ]
        )
    for c in copies + sum(blocks, []):
        c.start()
    for c in copies:
        c.wait()
    for i in range(NQ):
        at = pl.ds(i * BQ, BQ)
        for c in blocks[i]:
            c.wait()
        dn = nt(dhid[at, :], w[...])
        n = normed[at, :].astype(F32)
        r = stats[at, 4:5]
        mean = jnp.mean(dn, axis=-1, keepdims=True)
        cross = jnp.mean(dn * n, axis=-1, keepdims=True)
        res = (r * (dn - mean - n * cross)).astype(BF)
        to = pl.ds((i % 2) * BQ, BQ)

        @pl.when(h == i // 2)
        def _(res=res, to=to):
            own[to, :] = res

        @pl.when(h != i // 2)
        def _(res=res, to=to):
            other[to, :] = res


def input_grad(dhid, normed, stats, wag):
    return pl.pallas_call(
        input_kernel,
        out_shape=[shape((512, D), BF)] * 2,
        in_specs=[HB, ANY, VM, HB],
        out_specs=[VM, VM],
        scratch_shapes=[
            pltpu.VMEM((L, D), BF),
            pltpu.VMEM((L, D), BF),
            pltpu.VMEM((D, D), BF),
            pltpu.SemaphoreType.DMA((16,)),
        ],
        compiler_params=params(20),
        name="input_grad",
    )(dhid, normed, stats, wag)


def add_kernel(a, b, *outs):
    _, p, _ = unit_of()
    for k in range(4):
        at = rows(jnp.bitwise_xor(p, k) * 128, 128)
        outs[k][...] = (a[at, :].astype(F32) + b[at, :].astype(F32)).astype(BF)


def add_halves(a, b):
    return pl.pallas_call(
        add_kernel,
        out_shape=[shape((128, D), BF)] * 4,
        in_specs=[VM, VM],
        out_specs=[VM] * 4,
        compiler_params=params(16),
        name="add_halves",
    )(a, b)


def place_kernel(*refs):
    chunks, out, sem = refs[:4], refs[4], refs[5]
    run_copies(
        [
            pltpu.make_async_copy(chunks[k], out.at[jnp.bitwise_xor(lax.axis_index("x"), k)], sem.at[k])
            for k in range(4)
        ]
    )


def place(chunks):
    return pl.pallas_call(
        place_kernel,
        out_shape=shape((4, 128, D), BF),
        in_specs=[ANY] * 4,
        out_specs=VM,
        scratch_shapes=[pltpu.SemaphoreType.DMA((4,))],
        compiler_params=params(16),
        name="place",
    )(*chunks)


def finish_kernel(mine, theirs, w_in, w_out, bias):
    for core in range(2):

        @pl.when(lax.axis_index("core") == core)
        def _(core=core):
            for side, src in ((core, mine), (1 - core, theirs)):
                for t in range(8):
                    col = 512 * (t // 2) + 256 * side + 128 * (t % 2)
                    w_in[:, col : col + 128] = src[128 * t : 128 * t + 128, :].astype(F32) / 128.0
                    at = 1024 + 32 * t
                    row, col = 32 * (t // 4), 512 * side + 128 * (t % 4)
                    w_out[row : row + 32, col : col + 128] = (
                        src[at : at + 32, :].astype(F32) / 128.0
                    )
                tail = src[1280:1296, :].astype(F32)
                bias[side : side + 1, :] = (tail[0:1] + tail[1:2]) / 128.0


def finish(mine, theirs):
    return pl.pallas_call(
        finish_kernel,
        out_shape=[shape((128, 2 * D), F32), shape((64, D), F32), shape((2, 128), F32)],
        in_specs=[VM, VM],
        out_specs=[VM] * 3,
        compiler_params=params(16),
        name="finish",
    )(mine, theirs)


def device(yh, core, yl, x):
    return ((yh * 2 + core) * 2 + yl) * 4 + x


def unit_device(e, p, half):
    ye, ce = e >> 1, e & 1
    yp, cp = p >> 1, p & 1
    return device(ye, half, yp, 2 * (ye ^ cp) + ce)


def input_pairs(k):
    pairs = []
    for p in range(4):
        for yl in range(2):
            for x in range(4):
                pairs.append((device(p >> 1, p & 1, yl, x), unit_device(x ^ k, p, yl)))
    return pairs


def grad_pairs(k):
    pairs = []
    for e in range(4):
        for yl in range(2):
            for x in range(4):
                pairs.append((device(e >> 1, e & 1, yl, x), unit_device(e, x ^ k, yl)))
    return pairs


def back_pairs(k):
    return [(b, a) for a, b in grad_pairs(k)]


def local(layer_in, repack_plan, lengths, stamps, w_in, w_out, time_bias, grad_out):
    first = lax.axis_index("core") == 0
    swap = functools.partial(lax.ppermute, axis_name="core", perm=[(0, 1), (1, 0)])

    wag = lax.all_gather(own_weights(w_in, w_out), "z", axis=0, tiled=True)
    chunks = deal(repack_plan, layer_in)
    xs = [lax.ppermute(c, PLANE, input_pairs(k)) for k, c in enumerate(chunks)]
    picked = pick(lengths, grad_out, stamps)
    gs = [lax.ppermute(c, PLANE, grad_pairs(k)) for k, c in enumerate(picked)]
    xs = xs + [swap(c) for c in xs]
    gs = gs + [swap(c) for c in gs]
    w3 = wag.reshape(8, 160, D)
    wrecv = swap(jnp.where(first, w3[4:, 128:], w3[:4, 128:]))

    normed, act, slope, probs, pslope, mixed, base = forward(time_bias, xs, gs, wag)
    dz, stats = statistics(mixed, act, base, gs, wag, wrecv)
    datt, dhu, keep, send = middle(stats, swap(stats), mixed, dz, act, slope, gs)
    part, dhid = backward(
        act, slope, probs, pslope, normed, datt, dhu, stats, keep, swap(send)
    )
    mine = lax.psum_scatter(part, "z", scatter_dimension=0, tiled=True)
    own, other = input_grad(dhid, normed, stats, wag)
    pieces = add_halves(own, swap(other))
    back = [lax.ppermute(pieces[k], PLANE, back_pairs(k)) for k in range(4)]
    input_gradient = place(back)
    mine, input_gradient = lax.optimization_barrier((mine, input_gradient))

    def exchange(v):
        return lax.all_to_all(v, CHIPS, split_axis=0, concat_axis=0, tiled=True)

    mine = jnp.pad(mine, ((0, SHARD - SENT), (0, 0)))
    spread = exchange(mine.reshape(16, SHARD // 16, 128))
    summed = jnp.sum(spread.astype(F32), axis=0, keepdims=True).astype(BF)
    mine = exchange(jnp.broadcast_to(summed, spread.shape)).reshape(SHARD, 128)
    grad_w_in, grad_w_out, grad_bias = finish(mine, swap(mine))
    return input_gradient, grad_w_in, grad_w_out, grad_bias


def solution(mesh):
    fine = Mesh(mesh.devices.reshape(2, 2, 2, 4, 8), ("yh", "core", "yl", "x", "z"))
    events = P(("yh", "core", "z"), ("yl", "x"), None)
    slots = P(("yh", "core", "z"))
    return jax.shard_map(
        local,
        mesh=fine,
        in_specs=(
            events,
            slots,
            slots,
            P(("yh", "core", "z"), ("yl", "x")),
            P("z", None),
            P("z", None),
            P(),
            events,
        ),
        out_specs=(events, P("z", None), P("z", None), P()),
        check_vma=False,
    )
```
